256 devices in a mesh: seq: 32 (over y, x, core), exp: 8 (over z).
Axes of the slice: x: 4, y: 4, z: 8, core: 2. Of those that a mesh axis runs over, the one named last changes fastest.
Arguments:
- patches: bfloat16 [2, 16384, 4096], P(None, 'seq', 'exp'), may hold values from -32 to 32
- grad_out: bfloat16 [2, 16384, 4096], P(None, 'seq', 'exp'), may hold values from -6 to 6
- phi_t: bfloat16 [16, 4096], P(None, 'exp'), may hold values from -0.0625 to 0.0625
- w_in: bfloat16 [8, 4096, 8192], P('exp', None, 'seq'), may hold values from -0.09375 to 0.09375
- w_out: bfloat16 [8, 8192, 4096], P('exp', 'seq'), may hold values from -0.0625 to 0.0625
Outputs:
- grad_patches: bfloat16 [2, 16384, 4096], P(None, 'seq', 'exp')
- grad_phi: float32 [16, 4096], P(None, 'exp')
- grad_w_in: bfloat16 [8, 4096, 8192], P('exp', None, 'seq')
- grad_w_out: bfloat16 [8, 8192, 4096], P('exp', 'seq')
The draws below stay inside these ranges and needn't reach their ends.
All inputs are finite; a program needn't handle non-finite values.
Results may differ from the reference program's by a relative error of at most 0.015.
Values may be sent and summed in bfloat16 or wider, within the bound.
A program may use at most 64 MiB of HBM per device.

```python
import math
import jax
import jax.numpy as jnp
from jax import lax

D = 4096
FF = 8192
SLOT_PER = 2
IMAGES = 2
PATCHES = 16384
EXPERTS = 8
SLOTS = 16


def phi_table(key):
    base = jax.random.normal(jax.random.fold_in(key, 7), (SLOTS, D), jnp.float32)
    return jnp.clip(base, -4.0, 4.0) / jnp.sqrt(jnp.float32(D))


def draw_phi_t(key, part):
    return phi_table(key).astype(jnp.bfloat16)


def draw_patches(key, part):
    noise = jax.random.normal(jax.random.fold_in(key, 11), (IMAGES, PATCHES, D), jnp.float32)
    ramp = 0.6 + 1.2 * jnp.arange(PATCHES, dtype=jnp.float32) / PATCHES
    values = noise * ramp[None, :, None]
    return jnp.clip(values, -32.0, 32.0).astype(jnp.bfloat16)


def steps_of(key, shape, shards, low, top_value):
    def one(dim, shards_of):
        heights = jax.random.uniform(jax.random.fold_in(jax.random.fold_in(key, 6), dim), (shards_of,), jnp.float32, low / len(shards), top_value / len(shards))
        return jnp.repeat(jnp.exp(heights), shape[dim] // shards_of).reshape((-1,) + (1,) * (len(shape) - dim - 1))

    gain = one(*shards[0])
    for cut in shards[1:]:
        gain = gain * one(*cut)
    return gain


def normal_values(own_key, shape, spread, reach, shards=(), kind=jnp.bfloat16):
    level = steps_of(own_key, shape, shards, -0.22, 0.18) if shards else 1.0
    drawn = jax.random.normal(own_key, shape, jnp.float32) * spread * level
    return jnp.minimum(jnp.maximum(drawn, -reach), reach).astype(kind)


def setup_inputs(seed: int = 0) -> dict:
    splits = jax.random.split(jax.random.key(seed), 6)
    return {
        "patches": draw_patches(jax.random.fold_in(splits[5], 71), 0),
        "grad_out": normal_values(splits[1], (IMAGES, PATCHES, D), 1.0, 6.0, ((1, 32), (2, 8))),
        "phi_t": draw_phi_t(jax.random.fold_in(splits[5], 71), 0),
        "w_in": normal_values(splits[3], (EXPERTS, D, FF), D ** -0.5, 0.09375, ((0, 8), (2, 32))),
        "w_out": normal_values(splits[4], (EXPERTS, FF, D), FF ** -0.5, 0.0625, ((0, 8), (1, 32))),
    }


slope_coef = 0.7978845608
cubic_coef = 0.044715

def gelu_value(value):
    inner = slope_coef * (value + cubic_coef * value * value * value)
    return 0.5 * value * (1.0 + jnp.tanh(inner))

def gelu_slope(value):
    inner = slope_coef * (value + cubic_coef * value * value * value)
    tangent = jnp.tanh(inner)
    return 0.5 * (1.0 + tangent) + 0.5 * value * (1.0 - tangent * tangent) * slope_coef * (1.0 + 3.0 * cubic_coef * value * value)

def expert_pass(items):
    rows, grads, w_first, w_second = items
    hidden_pre = jnp.dot(rows, w_first, preferred_element_type=jnp.float32)
    active = gelu_value(hidden_pre).astype(jnp.bfloat16)
    outputs = jnp.dot(active, w_second, preferred_element_type=jnp.float32).astype(jnp.bfloat16)
    act_grad = jnp.dot(grads, w_second.T, preferred_element_type=jnp.float32)
    pre_grad = (act_grad * gelu_slope(hidden_pre)).astype(jnp.bfloat16)
    grad_second = jnp.dot(active.T, grads, preferred_element_type=jnp.float32).astype(jnp.bfloat16)
    grad_first = jnp.dot(rows.T, pre_grad, preferred_element_type=jnp.float32).astype(jnp.bfloat16)
    input_grad = jnp.dot(pre_grad, w_first.T, preferred_element_type=jnp.float32).astype(jnp.bfloat16)
    return (outputs, input_grad, grad_first, grad_second)

def reference(patches, grad_out, phi_t, w_in, w_out):
    images = patches.shape[0]
    width = patches.shape[2]
    count = w_in.shape[0]
    patch_f = patches.astype(jnp.float32)
    grad_f = grad_out.astype(jnp.float32)
    phi_f = phi_t.astype(jnp.float32)
    logits = jnp.einsum('ipd,sd->ips', patch_f, phi_f)
    dispatch = jax.nn.softmax(logits, axis=1)
    combine = jax.nn.softmax(logits, axis=2)
    dispatch_b = dispatch.astype(jnp.bfloat16)
    combine_b = combine.astype(jnp.bfloat16)
    slot_in = jnp.einsum('ips,ipd->isd', dispatch_b.astype(jnp.float32), patch_f).astype(jnp.bfloat16)
    slot_grad = jnp.einsum('ips,ipd->isd', combine_b.astype(jnp.float32), grad_f).astype(jnp.bfloat16)

    def to_experts(block):
        return block.reshape(images, count, SLOT_PER, width).transpose(1, 0, 2, 3).reshape(count, images * SLOT_PER, width)

    def from_experts(block):
        return block.reshape(count, images, SLOT_PER, width).transpose(1, 0, 2, 3).reshape(images, count * SLOT_PER, width)
    outputs, input_grad, grad_w_in, grad_w_out = lax.map(expert_pass, (to_experts(slot_in), to_experts(slot_grad), w_in, w_out))
    slot_out = from_experts(outputs).astype(jnp.float32)
    input_grad = from_experts(input_grad).astype(jnp.float32)
    comb_grad = jnp.einsum('ipd,isd->ips', grad_f, slot_out)
    disp_grad = jnp.einsum('ipd,isd->ips', patch_f, input_grad)
    row_dots = lax.optimization_barrier(jnp.sum(combine * comb_grad, axis=2, keepdims=True))
    col_dots = lax.optimization_barrier(jnp.sum(dispatch * disp_grad, axis=1, keepdims=True))
    logit_grad = combine * (comb_grad - row_dots) + dispatch * (disp_grad - col_dots)
    logit_b = logit_grad.astype(jnp.bfloat16).astype(jnp.float32)
    grad_patches = (jnp.einsum('ips,isd->ipd', dispatch_b.astype(jnp.float32), input_grad) + jnp.einsum('ips,sd->ipd', logit_b, phi_f)).astype(jnp.bfloat16)
    norm_factor = 1.0 / math.sqrt(images * patches.shape[1])
    grad_phi = jnp.einsum('ips,ipd->sd', logit_b, patch_f) * norm_factor
    return (grad_patches, grad_phi, grad_w_in, grad_w_out)
```

```python
import math

import jax
import jax.numpy as jnp
from jax import lax
from jax.experimental import pallas as pl
from jax.experimental.pallas import tpu as pltpu
from jax.sharding import PartitionSpec as P

MESH = pl.DeviceIdType.MESH
F32 = jnp.float32
BF16 = jnp.bfloat16

slope_coef = 0.7978845608
cubic_coef = 0.044715

NS = 32
NZ = 8
LANE = 128


def nn(a, b):
    return lax.dot_general(a, b, (((1,), (0,)), ((), ())), preferred_element_type=F32)


def nt(a, b):
    return lax.dot_general(a, b, (((1,), (1,)), ((), ())), preferred_element_type=F32)


def tn(a, b):
    return lax.dot_general(a, b, (((0,), (0,)), ((), ())), preferred_element_type=F32)


def iota(shape, dim):
    return lax.broadcasted_iota(jnp.int32, shape, dim)


def kernel(
    patches, grad_out, phi_t, w_in, w_out,
    grad_patches, grad_phi, grad_w_in, grad_w_out,
    pv, gv, phv, wiv, wov, gpv, gphv, gwiv, gwov,
    asend, arecv, logit, csend, crecv, dtmp, dsend, drecv, rows_f,
    esend, erecv, fsend, frecv, lse_b, gsend, grecv, hbuf, isend, irecv, jbuf,
    in_sem, out_sem, send_sem, recv_sem,
):
    r = lax.axis_index("seq")
    z = lax.axis_index("exp")
    owner = lax.rem(r, 16) // 2
    q = (r // 16) * 2 + lax.rem(r, 2)

    def tile_of(rr):
        return (lax.rem(rr, 16) // 2) * 4 + (rr // 16) * 2 + lax.rem(rr, 2)

    loads = [
        pltpu.make_async_copy(src, dst, in_sem.at[k])
        for k, (src, dst) in enumerate(
            [(phi_t, phv), (patches, pv), (grad_out, gv), (w_in, wiv), (w_out, wov)]
        )
    ]
    for load in loads:
        load.start()

    barrier = pltpu.get_barrier_semaphore()

    def greet(rr, zz):
        pl.semaphore_signal(barrier, inc=1, device_id=(rr, zz), device_id_type=MESH)

    @pl.loop(1, NZ)
    def _(k):
        greet(r, lax.rem(z + k, NZ))

    @pl.loop(1, NS)
    def _(k):
        greet(lax.rem(r + k, NS), z)

    for i in range(2):
        for sp in range(2):
            rr = i * 16 + 2 * z + sp

            @pl.when(rr != r)
            def _():
                @pl.loop(1, NZ)
                def _(k):
                    greet(rr, lax.rem(z + k, NZ))

    def remote(src, dst, phase, rr, zz):
        return pltpu.make_async_remote_copy(
            src_ref=src,
            dst_ref=dst,
            send_sem=send_sem.at[phase],
            recv_sem=recv_sem.at[phase],
            device_id=(rr, zz),
            device_id_type=MESH,
        )

    def arrived(ref, phase):
        pltpu.make_async_copy(ref, ref, recv_sem.at[phase]).wait()

    def sent(ref, phase):
        pltpu.make_async_copy(ref, ref, send_sem.at[phase]).wait()

    loads[0].wait()
    loads[1].wait()
    phi = phv[...]
    for i in range(2):
        part = nt(phi, pv[i])
        for b in range(4):
            asend[i * 4 + b] = part[:, b * LANE : (b + 1) * LANE]

    extra = jnp.where(owner == z, 0, NS - 1)
    pl.semaphore_wait(barrier, NZ - 1 + NS - 1 + extra)

    @pl.loop(1, NZ)
    def _(k):
        zz = lax.rem(z + k, NZ)
        remote(asend.at[zz], arecv.at[z], 0, r, zz).start()

    arecv[z] = asend[z]
    arrived(arecv.at[pl.ds(0, NZ - 1)], 0)
    total = arecv[0]
    for k in range(1, NZ):
        total = total + arecv[k]
    logit[z] = total

    @pl.loop(1, NZ)
    def _(k):
        zz = lax.rem(z + k, NZ)
        remote(logit.at[z], logit.at[z], 1, r, zz).start()

    arrived(logit.at[pl.ds(0, NZ - 1)], 1)
    loads[2].wait()

    diag = iota((32, LANE), 0) == iota((32, LANE), 1)
    peaks, sums = [], []
    for i in range(2):
        li = jnp.concatenate([logit[i * 4 + b] for b in range(4)], axis=1)
        peak = jnp.max(li, axis=1, keepdims=True)
        e = jnp.exp(li - peak)
        peaks.append(peak)
        sums.append(jnp.sum(e, axis=1, keepdims=True))
        hi = e.astype(BF16)
        lo = (e - hi.astype(F32)).astype(BF16)
        both = nn(jnp.concatenate([hi, lo], axis=0), pv[i])
        slot_part = both[:16] + both[16:]
        ec = jnp.exp(li - jnp.max(li, axis=0, keepdims=True))
        combine_b = (ec / jnp.sum(ec, axis=0, keepdims=True)).astype(BF16)
        grad_part = nn(combine_b, gv[i])
        for half in range(2):
            for c in range(4):
                base = (i * 16 + half * 8) * 16 + c
                rows = slice(half * 8, half * 8 + 8)
                lanes = slice(c * LANE, (c + 1) * LANE)
                csend[pl.ds(base, 8, stride=16), :] = slot_part[rows, lanes]
                csend[pl.ds(base + 4, 8, stride=16), :] = grad_part[rows, lanes]
    peak_col = jnp.concatenate(peaks, axis=0)
    sum_col = jnp.concatenate(sums, axis=0)
    peak_row = jnp.sum(jnp.where(diag, peak_col, 0.0), axis=0, keepdims=True)
    sum_row = jnp.sum(jnp.where(diag, sum_col, 0.0), axis=0, keepdims=True)
    csend[pl.ds(8, 32, stride=16), :] = jnp.broadcast_to(peak_row, (32, LANE))
    csend[pl.ds(9, 32, stride=16), :] = jnp.broadcast_to(sum_row, (32, LANE))

    mine = pl.ds(pl.multiple_of(r * 16, 16), 16)

    @pl.loop(1, NS)
    def _(k):
        rr = lax.rem(r + k, NS)
        there = pl.ds(pl.multiple_of(rr * 16, 16), 16)
        remote(csend.at[there], crecv.at[mine], 2, rr, z).start()

    crecv[mine, :] = csend[mine, :]
    arrived(crecv.at[pl.ds(0, 16 * (NS - 1))], 2)

    peak_all = crecv[pl.ds(8, 32, stride=16), :]
    sum_all = crecv[pl.ds(9, 32, stride=16), :]
    top = jnp.max(peak_all, axis=0, keepdims=True)
    scale = jnp.exp(peak_all - top)
    denom = jnp.sum(scale * sum_all, axis=0, keepdims=True)
    lse_row = top + jnp.log(denom)
    lse_col = jnp.sum(jnp.where(diag, lse_row, 0.0), axis=1, keepdims=True)
    lse_b[...] = jnp.broadcast_to(lse_col, (32, LANE))
    weight = jnp.sum(
        jnp.where(iota((32, LANE), 1) == r, scale / denom, 0.0), axis=1, keepdims=True
    )
    dtmp[...] = jnp.zeros((16, LANE), F32)
    for c in range(4):
        row = jnp.sum(weight * crecv[pl.ds(c, 32, stride=16), :], axis=0, keepdims=True)
        high = row.astype(BF16).astype(F32)
        dtmp[c : c + 1, :] = high
        dtmp[4 + c : 5 + c, :] = row - high
        dtmp[8 + c : 9 + c, :] = jnp.sum(
            crecv[pl.ds(4 + c, 32, stride=16), :], axis=0, keepdims=True
        )
    dsend[...] = dtmp[...].astype(BF16)

    dplace = drecv.at[
        pl.ds(pl.multiple_of(q * 16, 16), 16), pl.ds(pl.multiple_of(z * LANE, LANE), LANE)
    ]

    @pl.when(owner != z)
    def _():
        remote(dsend, dplace, 3, r, owner).start()

    @pl.when(owner == z)
    def _():
        pltpu.make_async_copy(dsend, dplace, recv_sem.at[3]).start()

    @pl.loop(1, NS)
    def _(k):
        remote(dsend, dplace, 3, lax.rem(r + k, NS), owner).start()

    at = iota((96, 64), 0)
    c_of, j = at // 24, lax.rem(at, 24)
    part_of = jnp.where(j < 8, 0, jnp.where(j < 16, 8, 4))
    want = lax.rem(j, 4) * 16 + part_of + c_of
    pick = jnp.where(iota((96, 64), 1) == want, 1.0, 0.0).astype(BF16)

    arrived(drecv, 3)
    picked = nn(pick, drecv[...])
    for c in range(4):
        for b in range(NZ):
            rows_f[:, (b * 4 + c) * LANE : (b * 4 + c + 1) * LANE] = picked[
                c * 24 : c * 24 + 24, b * LANE : (b + 1) * LANE
            ]
    loads[3].wait()
    loads[4].wait()
    lhs = rows_f[0:16, :].astype(BF16)
    hidden = nn(lhs, wiv[0])[0:8]
    act_grad = nt(lhs, wov[0])[8:16]
    inner = slope_coef * (hidden + cubic_coef * hidden * hidden * hidden)
    tangent = jnp.tanh(inner)
    active = 0.5 * hidden * (1.0 + tangent)
    slope = 0.5 * (1.0 + tangent) + 0.5 * hidden * (1.0 - tangent * tangent) * slope_coef * (
        1.0 + 3.0 * cubic_coef * hidden * hidden
    )
    pre = act_grad * slope
    upper = iota((8, 256), 0) < 4
    none = jnp.zeros((8, 256), F32)
    active = jnp.where(upper, active, 0.0)
    pre = jnp.where(upper, 0.0, pre)
    active_lo = jnp.concatenate([active, none], axis=0).astype(BF16)
    active_hi = jnp.concatenate([none, active], axis=0).astype(BF16)
    pre_lo = jnp.concatenate([pre, none], axis=0).astype(BF16)
    esend[...] = (nn(active_lo, wov[0]) + nt(pre_lo, wiv[0]))[0:8]

    own = pl.ds(pl.multiple_of(tile_of(r) * LANE, LANE), LANE)

    @pl.loop(1, NS)
    def _(k):
        rr = lax.rem(r + k, NS)
        lanes = pl.ds(pl.multiple_of(tile_of(rr) * LANE, LANE), LANE)
        remote(esend.at[:, lanes], erecv.at[r], 4, rr, z).start()

    erecv[r] = esend[:, own]

    gwov[0] = tn(active_hi, lhs).astype(BF16)
    gwiv[0] = tn(lhs, pre_lo).astype(BF16)
    stores = [
        pltpu.make_async_copy(gwiv, grad_w_in, out_sem.at[0]),
        pltpu.make_async_copy(gwov, grad_w_out, out_sem.at[1]),
    ]
    for store in stores:
        store.start()

    arrived(erecv.at[pl.ds(0, NS - 1)], 4)
    total = erecv[0]
    for k in range(1, NS):
        total = total + erecv[k]
    total = total.astype(BF16).astype(F32)
    slot_in = rows_f[0:8, own] + rows_f[16:24, own]
    product = total * slot_in
    high = product.astype(BF16).astype(F32)
    rest = pltpu.roll(product - high, 4, 0)
    fsend[...] = jnp.concatenate(
        [total, jnp.where(iota((8, LANE), 0) < 4, rest, high)], axis=0
    ).astype(BF16)

    fplace = frecv.at[
        pl.ds(pl.multiple_of(z * 16, 16), 16), pl.ds(pl.multiple_of(q * LANE, LANE), LANE)
    ]

    @pl.when(owner != z)
    def _():
        remote(fsend, fplace, 5, r, owner).start()

    @pl.when(owner == z)
    def _():
        pltpu.make_async_copy(fsend, fplace, recv_sem.at[5]).start()

    @pl.loop(1, NS)
    def _(k):
        remote(fsend, fplace, 5, lax.rem(r + k, NS), owner).start()

    at = iota((96, LANE), 0)
    kind, slot = at // 32, lax.rem(at, 16)
    want = (slot // 2) * 16 + kind * 4 + (lax.rem(at, 32) // 16) * 2 + lax.rem(slot, 2)
    col = iota((96, LANE), 1)
    pick = jnp.where(
        (col == want) | ((kind == 2) & (col == want + 4)), 1.0, 0.0
    ).astype(BF16)

    arrived(frecv, 5)
    picked = nn(pick, frecv[...])
    slot_out = picked[0:32].astype(BF16)
    input_grad = picked[32:64].astype(BF16)
    col_part = jnp.sum(picked[64:96], axis=1, keepdims=True)
    for i in range(2):
        rows = slice(i * 16, i * 16 + 16)
        comb_part = nt(slot_out[rows], gv[i])
        disp_part = nt(input_grad[rows], pv[i]) - col_part[rows]
        for b in range(4):
            lanes = slice(b * LANE, (b + 1) * LANE)
            gsend[i * 4 + b, 0:16] = comb_part[:, lanes]
            gsend[i * 4 + b, 16:32] = disp_part[:, lanes]

    @pl.loop(1, NZ)
    def _(k):
        zz = lax.rem(z + k, NZ)
        remote(gsend.at[zz], grecv.at[z], 6, r, zz).start()

    grecv[z] = gsend[z]
    chunk = logit[z]
    ec = jnp.exp(chunk - jnp.max(chunk, axis=0, keepdims=True))
    combine = ec / jnp.sum(ec, axis=0, keepdims=True)
    dispatch = jnp.exp(chunk - lse_b[pl.ds(pl.multiple_of((z // 4) * 16, 16), 16), :])
    arrived(grecv.at[pl.ds(0, NZ - 1)], 6)
    total = grecv[0]
    for k in range(1, NZ):
        total = total + grecv[k]
    comb_grad, disp_grad = total[0:16], total[16:32]
    row_dots = jnp.sum(combine * comb_grad, axis=0, keepdims=True)
    hbuf[z] = (combine * (comb_grad - row_dots) + dispatch * disp_grad).astype(BF16)

    @pl.loop(1, NZ)
    def _(k):
        zz = lax.rem(z + k, NZ)
        remote(hbuf.at[z], hbuf.at[z], 7, r, zz).start()

    dispatch_b = []
    for i in range(2):
        li = jnp.concatenate([logit[i * 4 + b] for b in range(4)], axis=1)
        dispatch_b.append(jnp.exp(li - lse_col[i * 16 : i * 16 + 16]).astype(BF16))
    arrived(hbuf.at[pl.ds(0, NZ - 1)], 7)
    logit_b = [
        jnp.concatenate([hbuf[i * 4 + b] for b in range(4)], axis=1) for i in range(2)
    ]
    phi_part = nn(logit_b[0], pv[0]) + nn(logit_b[1], pv[1])
    for u in range(8):
        half, c = u // 4, u % 4
        isend[u] = phi_part[half * 8 : half * 8 + 8, c * LANE : (c + 1) * LANE]

    @pl.loop(0, 8)
    def _(u):
        @pl.when(4 * u != r)
        def _():
            remote(isend.at[u], irecv.at[r], 8, 4 * u, z).start()

    for i in range(2):
        left = jnp.concatenate([dispatch_b[i], logit_b[i]], axis=0)
        right = jnp.concatenate([input_grad[i * 16 : i * 16 + 16], phi], axis=0)
        gpv[i] = tn(left, right).astype(BF16)
    stores.append(pltpu.make_async_copy(gpv, grad_patches, out_sem.at[2]))
    stores[2].start()

    tile = r // 4

    @pl.when(lax.rem(r, 4) == 0)
    def _():
        irecv[r] = isend[tile]
        arrived(irecv.at[pl.ds(0, NS - 1)], 8)
        total = irecv[0]
        for k in range(1, NS):
            total = total + irecv[k]
        jbuf[tile] = total * (1.0 / math.sqrt(2 * 512 * NS))

        @pl.loop(1, NS)
        def _(k):
            remote(jbuf.at[tile], jbuf.at[tile], 9, lax.rem(r + k, NS), z).start()

        arrived(jbuf.at[pl.ds(0, 7)], 9)
        sent(irecv.at[pl.ds(0, NS - 1)], 9)
        sent(isend.at[pl.ds(0, 7)], 8)

    @pl.when(lax.rem(r, 4) != 0)
    def _():
        arrived(jbuf, 9)
        sent(isend, 8)

    for u in range(8):
        half, c = u // 4, u % 4
        gphv[half * 8 : half * 8 + 8, c * LANE : (c + 1) * LANE] = jbuf[u]
    stores.append(pltpu.make_async_copy(gphv, grad_phi, out_sem.at[3]))
    stores[3].start()

    sent(asend.at[pl.ds(0, NZ - 1)], 0)
    sent(logit.at[pl.ds(0, NZ - 1)], 1)
    sent(csend.at[pl.ds(0, 16 * (NS - 1))], 2)
    sent(esend.at[:, pl.ds(0, LANE * (NS - 1))], 4)
    sent(gsend.at[pl.ds(0, NZ - 1)], 6)
    sent(hbuf.at[pl.ds(0, NZ - 1)], 7)

    @pl.when(owner == z)
    def _():
        sent(drecv.at[:, pl.ds(0, 7 * LANE)], 3)
        sent(drecv.at[pl.ds(0, 48), pl.ds(0, LANE)], 3)
        sent(frecv.at[:, pl.ds(0, 3 * LANE)], 5)
        sent(frecv.at[pl.ds(0, 112), pl.ds(0, LANE)], 5)

    @pl.when(owner != z)
    def _():
        sent(drecv, 3)
        sent(frecv, 5)

    for store in stores:
        store.wait()


def local(patches, grad_out, phi_t, w_in, w_out):
    anywhere = pl.BlockSpec(memory_space=pl.ANY)
    vmem = pltpu.VMEM
    return pl.pallas_call(
        kernel,
        out_shape=(
            jax.ShapeDtypeStruct(patches.shape, BF16),
            jax.ShapeDtypeStruct(phi_t.shape, F32),
            jax.ShapeDtypeStruct(w_in.shape, BF16),
            jax.ShapeDtypeStruct(w_out.shape, BF16),
        ),
        in_specs=[anywhere] * 5,
        out_specs=[anywhere] * 4,
        scratch_shapes=[
            vmem((2, 512, 512), BF16),
            vmem((2, 512, 512), BF16),
            vmem((16, 512), BF16),
            vmem((1, 4096, 256), BF16),
            vmem((1, 256, 4096), BF16),
            vmem((2, 512, 512), BF16),
            vmem((16, 512), F32),
            vmem((1, 4096, 256), BF16),
            vmem((1, 256, 4096), BF16),
            vmem((8, 16, LANE), F32),
            vmem((8, 16, LANE), F32),
            vmem((8, 16, LANE), F32),
            vmem((512, LANE), F32),
            vmem((512, LANE), F32),
            vmem((16, LANE), F32),
            vmem((16, LANE), BF16),
            vmem((64, 1024), BF16),
            vmem((24, 4096), F32),
            vmem((8, 4096), F32),
            vmem((32, 8, LANE), F32),
            vmem((16, LANE), BF16),
            vmem((LANE, 512), BF16),
            vmem((32, LANE), F32),
            vmem((8, 32, LANE), F32),
            vmem((8, 32, LANE), F32),
            vmem((8, 16, LANE), BF16),
            vmem((8, 8, LANE), F32),
            vmem((32, 8, LANE), F32),
            vmem((8, 8, LANE), F32),
            pltpu.SemaphoreType.DMA((5,)),
            pltpu.SemaphoreType.DMA((4,)),
            pltpu.SemaphoreType.DMA((10,)),
            pltpu.SemaphoreType.DMA((10,)),
        ],
        compiler_params=pltpu.CompilerParams(
            collective_id=0, has_side_effects=True, vmem_limit_bytes=48 * 1024 * 1024
        ),
        cost_estimate=pl.CostEstimate(
            flops=400_000_000, bytes_accessed=12_000_000, transcendentals=100_000
        ),
    )(patches, grad_out, phi_t, w_in, w_out)


def solution(mesh):
    in_specs = (
        P(None, "seq", "exp"),
        P(None, "seq", "exp"),
        P(None, "exp"),
        P("exp", None, "seq"),
        P("exp", "seq", None),
    )
    out_specs = (
        P(None, "seq", "exp"),
        P(None, "exp"),
        P("exp", None, "seq"),
        P("exp", "seq", None),
    )
    return jax.shard_map(local, mesh=mesh, in_specs=in_specs, out_specs=out_specs, check_vma=False)
```

```python
import math

import jax
import jax.numpy as jnp
from jax import lax
from jax.experimental import pallas as pl
from jax.experimental.pallas import tpu as pltpu
from jax.sharding import PartitionSpec as P

MESH = pl.DeviceIdType.MESH
F32 = jnp.float32
BF16 = jnp.bfloat16

slope_coef = 0.7978845608
cubic_coef = 0.044715

NS = 32
NZ = 8
LANE = 128


def nn(a, b):
    return lax.dot_general(a, b, (((1,), (0,)), ((), ())), preferred_element_type=F32)


def nt(a, b):
    return lax.dot_general(a, b, (((1,), (1,)), ((), ())), preferred_element_type=F32)


def tn(a, b):
    return lax.dot_general(a, b, (((0,), (0,)), ((), ())), preferred_element_type=F32)


def iota(shape, dim):
    return lax.broadcasted_iota(jnp.int32, shape, dim)


def thirds(value):
    first = value.astype(BF16).astype(F32)
    second = (value - first).astype(BF16).astype(F32)
    return first, second, value - first - second


def spread(column):
    first, second, third = thirds(column)
    lane = iota((8, LANE), 1)
    return jnp.where(
        lane == 0, first, jnp.where(lane == 1, second, jnp.where(lane == 2, third, 0.0))
    )


def kernel(
    patches, grad_out, phi_t, w_in, w_out,
    grad_patches, grad_phi, grad_w_in, grad_w_out,
    pv, gv, phv, wiv, wov, gpv, gphv, gwiv, gwov,
    asend, arecv, logit, cfull, csend, crecv, dtmp, dsend, drecv, rows_f,
    esend, erecv, fsend, frecv, lse_b, dots_b, gsend, grecv, hbuf, isend, irecv, jbuf,
    in_sem, out_sem, send_sem, recv_sem,
):
    r = lax.axis_index("seq")
    z = lax.axis_index("exp")
    source, q = r // 4, lax.rem(r, 4)

    loads = [
        pltpu.make_async_copy(src, dst, in_sem.at[k])
        for k, (src, dst) in enumerate(
            [(phi_t, phv), (patches, pv), (grad_out, gv), (w_in, wiv), (w_out, wov)]
        )
    ]
    for load in loads:
        load.start()

    barrier = pltpu.get_barrier_semaphore()

    def greet(rr, zz):
        pl.semaphore_signal(barrier, inc=1, device_id=(rr, zz), device_id_type=MESH)

    @pl.loop(1, NZ)
    def _(k):
        greet(r, lax.rem(z + k, NZ))

    @pl.loop(1, NS)
    def _(k):
        greet(lax.rem(r + k, NS), z)

    @pl.when(source != z)
    def _():
        @pl.loop(1, NS)
        def _(k):
            greet(lax.rem(r + k, NS), source)

    def remote(src, dst, phase, rr, zz):
        return pltpu.make_async_remote_copy(
            src_ref=src,
            dst_ref=dst,
            send_sem=send_sem.at[phase],
            recv_sem=recv_sem.at[phase],
            device_id=(rr, zz),
            device_id_type=MESH,
        )

    def arrived(ref, phase):
        pltpu.make_async_copy(ref, ref, recv_sem.at[phase]).wait()

    dwait = fwait = csend.at[pl.ds(0, 16 * (NS - 1))]

    def sent(ref, phase):
        pltpu.make_async_copy(ref, ref, send_sem.at[phase]).wait()

    def scatter(piece, place, phase):
        @pl.loop(0, NS)
        def _(k):
            e, qq = lax.rem(z + 1 + k // 4, NZ), lax.rem(r + k, 4)
            rr = z * 4 + qq

            @pl.when((rr != r) | (e != z))
            def _():
                remote(piece(qq, e), place, phase, rr, e).start()

            @pl.when((rr == r) & (e == z))
            def _():
                pltpu.make_async_copy(piece(qq, e), place, recv_sem.at[phase]).start()

    loads[0].wait()
    loads[1].wait()
    phi = phv[...]
    for i in range(2):
        part = nt(phi, pv[i])
        for b in range(4):
            asend[i * 4 + b] = part[:, b * LANE : (b + 1) * LANE]

    extra = jnp.where(source == z, 3 * (NZ - 1), 4 * (NZ - 1))
    pl.semaphore_wait(barrier, NZ - 1 + NS - 1 + extra)

    @pl.loop(1, NZ)
    def _(k):
        zz = lax.rem(z + k, NZ)
        remote(asend.at[zz], arecv.at[z], 0, r, zz).start()

    arecv[z] = asend[z]
    arrived(arecv.at[pl.ds(0, NZ - 1)], 0)
    total = arecv[0]
    for k in range(1, NZ):
        total = total + arecv[k]
    logit[z] = total

    @pl.loop(1, NZ)
    def _(k):
        zz = lax.rem(z + k, NZ)
        remote(logit.at[z], logit.at[z], 1, r, zz).start()

    arrived(logit.at[pl.ds(0, NZ - 1)], 1)
    loads[2].wait()

    diag = iota((32, LANE), 0) == iota((32, LANE), 1)
    peaks, sums = [], []
    for i in range(2):
        li = jnp.concatenate([logit[i * 4 + b] for b in range(4)], axis=1)
        peak = jnp.max(li, axis=1, keepdims=True).astype(BF16).astype(F32)
        e = jnp.exp(li - peak)
        peaks.append(peak)
        sums.append(jnp.sum(e, axis=1, keepdims=True))
        hi = e.astype(BF16)
        lo = (e - hi.astype(F32)).astype(BF16)
        both = nn(jnp.concatenate([hi, lo], axis=0), pv[i])
        slot_part = both[:16] + both[16:]
        ec = jnp.exp(li - jnp.max(li, axis=0, keepdims=True))
        combine_b = (ec / jnp.sum(ec, axis=0, keepdims=True)).astype(BF16)
        grad_part = nn(combine_b, gv[i])
        for half in range(2):
            for c in range(4):
                base = (i * 16 + half * 8) * 16 + c
                rows = slice(half * 8, half * 8 + 8)
                lanes = slice(c * LANE, (c + 1) * LANE)
                high = slot_part[rows, lanes].astype(BF16).astype(F32)
                cfull[pl.ds(base, 8, stride=16), :] = high
                cfull[pl.ds(base + 4, 8, stride=16), :] = slot_part[rows, lanes] - high
                cfull[pl.ds(base + 8, 8, stride=16), :] = grad_part[rows, lanes]
    peak_col = jnp.concatenate(peaks, axis=0)
    sum_col = jnp.concatenate(sums, axis=0)
    peak_row = jnp.sum(jnp.where(diag, peak_col, 0.0), axis=0, keepdims=True)
    sum_row = jnp.sum(jnp.where(diag, sum_col, 0.0), axis=0, keepdims=True)
    stats = (peak_row,) + thirds(sum_row)
    for k, row in enumerate(stats):
        cfull[pl.ds(12 + k, 32, stride=16), :] = jnp.broadcast_to(row, (32, LANE))
    csend[...] = cfull[...].astype(BF16)

    def piece(qq, e):
        row = (qq // 2) * 16 + e * 2 + lax.rem(qq, 2)
        return csend.at[pl.ds(pl.multiple_of(row * 16, 16), 16)]

    scatter(piece, crecv.at[pl.ds(pl.multiple_of(r * 16, 16), 16)], 2)
    arrived(crecv, 2)
    cfull[...] = crecv[...].astype(F32)
    peak_all = cfull[pl.ds(12, 32, stride=16), :]
    sum_all = (
        cfull[pl.ds(13, 32, stride=16), :]
        + cfull[pl.ds(14, 32, stride=16), :]
        + cfull[pl.ds(15, 32, stride=16), :]
    )
    top = jnp.max(peak_all, axis=0, keepdims=True)
    scale = jnp.exp(peak_all - top)
    denom = jnp.sum(scale * sum_all, axis=0, keepdims=True)
    lse_row = top + jnp.log(denom)
    lse_col = jnp.sum(jnp.where(diag, lse_row, 0.0), axis=1, keepdims=True)
    lse_b[...] = jnp.broadcast_to(lse_col, (32, LANE))
    mine = (q // 2) * 16 + z * 2 + lax.rem(q, 2)
    weight = jnp.sum(
        jnp.where(iota((32, LANE), 1) == mine, scale / denom, 0.0), axis=1, keepdims=True
    )
    dtmp[...] = jnp.zeros((16, LANE), F32)
    for c in range(4):
        part = cfull[pl.ds(c, 32, stride=16), :] + cfull[pl.ds(4 + c, 32, stride=16), :]
        row = jnp.sum(weight * part, axis=0, keepdims=True)
        high = row.astype(BF16).astype(F32)
        dtmp[c : c + 1, :] = high
        dtmp[4 + c : 5 + c, :] = row - high
        dtmp[8 + c : 9 + c, :] = jnp.sum(
            cfull[pl.ds(8 + c, 32, stride=16), :], axis=0, keepdims=True
        )
    dsend[...] = dtmp[...].astype(BF16)

    drows = pl.ds(pl.multiple_of(q * 16, 16), 16)
    dlanes = pl.ds(pl.multiple_of(source * LANE, LANE), LANE)

    @pl.loop(1, NS)
    def _(k):
        remote(dsend, drecv.at[drows, dlanes], 3, lax.rem(r + k, NS), z).start()

    drecv[drows, dlanes] = dsend[...]

    at = iota((96, 64), 0)
    c_of, j = at // 24, lax.rem(at, 24)
    part_of = jnp.where(j < 8, 0, jnp.where(j < 16, 8, 4))
    want = lax.rem(j, 4) * 16 + part_of + c_of
    pick = jnp.where(iota((96, 64), 1) == want, 1.0, 0.0).astype(BF16)

    arrived(dwait, 3)
    picked = nn(pick, drecv[...])
    for c in range(4):
        for b in range(NZ):
            rows_f[:, (b * 4 + c) * LANE : (b * 4 + c + 1) * LANE] = picked[
                c * 24 : c * 24 + 24, b * LANE : (b + 1) * LANE
            ]
    loads[3].wait()
    loads[4].wait()
    lhs = rows_f[0:16, :].astype(BF16)
    hidden = nn(lhs, wiv[0])[0:8]
    act_grad = nt(lhs, wov[0])[8:16]
    inner = slope_coef * (hidden + cubic_coef * hidden * hidden * hidden)
    tangent = jnp.tanh(inner)
    active = 0.5 * hidden * (1.0 + tangent)
    slope = 0.5 * (1.0 + tangent) + 0.5 * hidden * (1.0 - tangent * tangent) * slope_coef * (
        1.0 + 3.0 * cubic_coef * hidden * hidden
    )
    pre = act_grad * slope
    upper = iota((8, 256), 0) < 4
    none = jnp.zeros((8, 256), F32)
    active = jnp.where(upper, active, 0.0)
    pre = jnp.where(upper, 0.0, pre)
    active_lo = jnp.concatenate([active, none], axis=0).astype(BF16)
    active_hi = jnp.concatenate([none, active], axis=0).astype(BF16)
    pre_lo = jnp.concatenate([pre, none], axis=0).astype(BF16)
    result = (nn(active_lo, wov[0]) + nt(pre_lo, wiv[0]))[0:8]
    wide = iota((8, 4096), 0) < 4
    dots = jnp.sum(result * (rows_f[0:8, :] + rows_f[16:24, :]), axis=1, keepdims=True)
    high = result.astype(BF16).astype(F32)
    rest = pltpu.roll(result - high, 4, 0)
    esend[...] = jnp.concatenate(
        [high, jnp.where(wide, rest, jnp.concatenate([spread(dots)] * 32, axis=1))], axis=0
    ).astype(BF16)

    def block(qq, e):
        return esend.at[:, pl.ds(pl.multiple_of((e * 4 + qq) * LANE, LANE), LANE)]

    scatter(block, erecv.at[r], 4)

    gwov[0] = tn(active_hi, lhs).astype(BF16)
    gwiv[0] = tn(lhs, pre_lo).astype(BF16)
    stores = [
        pltpu.make_async_copy(gwiv, grad_w_in, out_sem.at[0]),
        pltpu.make_async_copy(gwov, grad_w_out, out_sem.at[1]),
    ]
    for store in stores:
        store.start()

    arrived(erecv, 4)
    total = erecv[0].astype(F32)
    for k in range(1, NS):
        total = total + erecv[k].astype(F32)
    lower = iota((8, LANE), 0) < 4
    rest = pltpu.roll(total[8:16], 4, 0)
    dots = spread(jnp.sum(rest, axis=1, keepdims=True))
    fsend[...] = jnp.concatenate(
        [jnp.where(lower, total[0:8], total[0:8] + rest), jnp.where(lower, dots, 0.0)], axis=0
    ).astype(BF16)

    frows = pl.ds(pl.multiple_of(source * 16, 16), 16)
    flanes = pl.ds(pl.multiple_of(q * LANE, LANE), LANE)

    @pl.loop(1, NS)
    def _(k):
        remote(fsend, frecv.at[frows, flanes], 5, lax.rem(r + k, NS), z).start()

    frecv[frows, flanes] = fsend[...]

    at = iota((96, LANE), 0)
    kind, slot = at // 32, lax.rem(at, 16)
    want = (slot // 2) * 16 + kind * 4 + (lax.rem(at, 32) // 16) * 2 + lax.rem(slot, 2)
    col = iota((96, LANE), 1)
    pick = jnp.where(col == want, 1.0, 0.0).astype(BF16)

    arrived(fwait, 5)
    picked = nn(pick, frecv[...])
    slot_out = picked[0:32].astype(BF16)
    input_grad = picked[32:64].astype(BF16)
    dots_b[...] = jnp.broadcast_to(jnp.sum(picked[64:96, 0:LANE], axis=1, keepdims=True), (32, LANE))
    for i in range(2):
        rows = slice(i * 16, i * 16 + 16)
        comb_part = nt(slot_out[rows], gv[i])
        disp_part = nt(input_grad[rows], pv[i])
        for b in range(4):
            lanes = slice(b * LANE, (b + 1) * LANE)
            gsend[i * 4 + b, 0:16] = comb_part[:, lanes]
            gsend[i * 4 + b, 16:32] = disp_part[:, lanes]

    @pl.loop(1, NZ)
    def _(k):
        zz = lax.rem(z + k, NZ)
        remote(gsend.at[zz], grecv.at[z], 6, r, zz).start()

    grecv[z] = gsend[z]
    chunk = logit[z]
    ec = jnp.exp(chunk - jnp.max(chunk, axis=0, keepdims=True))
    combine = ec / jnp.sum(ec, axis=0, keepdims=True)
    image = pl.ds(pl.multiple_of((z // 4) * 16, 16), 16)
    dispatch = jnp.exp(chunk - lse_b[image, :])
    col_dots = dots_b[image, :]
    arrived(grecv.at[pl.ds(0, NZ - 1)], 6)
    total = grecv[0]
    for k in range(1, NZ):
        total = total + grecv[k]
    comb_grad, disp_grad = total[0:16], total[16:32]
    row_dots = jnp.sum(combine * comb_grad, axis=0, keepdims=True)
    hbuf[z] = (combine * (comb_grad - row_dots) + dispatch * (disp_grad - col_dots)).astype(BF16)

    @pl.loop(1, NZ)
    def _(k):
        zz = lax.rem(z + k, NZ)
        remote(hbuf.at[z], hbuf.at[z], 7, r, zz).start()

    dispatch_b = []
    for i in range(2):
        li = jnp.concatenate([logit[i * 4 + b] for b in range(4)], axis=1)
        dispatch_b.append(jnp.exp(li - lse_col[i * 16 : i * 16 + 16]).astype(BF16))
    arrived(hbuf.at[pl.ds(0, NZ - 1)], 7)
    logit_b = [
        jnp.concatenate([hbuf[i * 4 + b] for b in range(4)], axis=1) for i in range(2)
    ]
    phi_part = nn(logit_b[0], pv[0]) + nn(logit_b[1], pv[1])
    for u in range(8):
        half, c = u // 4, u % 4
        isend[u] = phi_part[half * 8 : half * 8 + 8, c * LANE : (c + 1) * LANE]

    @pl.loop(0, 8)
    def _(u):
        @pl.when(4 * u != r)
        def _():
            remote(isend.at[u], irecv.at[r], 8, 4 * u, z).start()

    for i in range(2):
        left = jnp.concatenate([dispatch_b[i], logit_b[i]], axis=0)
        right = jnp.concatenate([input_grad[i * 16 : i * 16 + 16], phi], axis=0)
        gpv[i] = tn(left, right).astype(BF16)
    stores.append(pltpu.make_async_copy(gpv, grad_patches, out_sem.at[2]))
    stores[2].start()

    tile = r // 4

    @pl.when(lax.rem(r, 4) == 0)
    def _():
        irecv[r] = isend[tile]
        arrived(irecv.at[pl.ds(0, NS - 1)], 8)
        total = irecv[0]
        for k in range(1, NS):
            total = total + irecv[k]
        jbuf[tile] = total * (1.0 / math.sqrt(2 * 512 * NS))

        @pl.loop(1, NS)
        def _(k):
            remote(jbuf.at[tile], jbuf.at[tile], 9, lax.rem(r + k, NS), z).start()

        arrived(jbuf.at[pl.ds(0, 7)], 9)
        sent(irecv.at[pl.ds(0, NS - 1)], 9)
        sent(isend.at[pl.ds(0, 7)], 8)

    @pl.when(lax.rem(r, 4) != 0)
    def _():
        arrived(jbuf, 9)
        sent(isend, 8)

    for u in range(8):
        half, c = u // 4, u % 4
        gphv[half * 8 : half * 8 + 8, c * LANE : (c + 1) * LANE] = jbuf[u]
    stores.append(pltpu.make_async_copy(gphv, grad_phi, out_sem.at[3]))
    stores[3].start()

    sent(asend.at[pl.ds(0, NZ - 1)], 0)
    sent(logit.at[pl.ds(0, NZ - 1)], 1)
    sent(dwait, 3)
    sent(fwait, 5)
    sent(gsend.at[pl.ds(0, NZ - 1)], 6)
    sent(hbuf.at[pl.ds(0, NZ - 1)], 7)

    @pl.when(source == z)
    def _():
        sent(crecv.at[pl.ds(0, 16 * (NS - 1))], 2)
        sent(erecv.at[pl.ds(0, NS - 1)], 4)

    @pl.when(source != z)
    def _():
        sent(crecv, 2)
        sent(erecv, 4)

    for store in stores:
        store.wait()


def local(patches, grad_out, phi_t, w_in, w_out):
    anywhere = pl.BlockSpec(memory_space=pl.ANY)
    vmem = pltpu.VMEM
    return pl.pallas_call(
        kernel,
        out_shape=(
            jax.ShapeDtypeStruct(patches.shape, BF16),
            jax.ShapeDtypeStruct(phi_t.shape, F32),
            jax.ShapeDtypeStruct(w_in.shape, BF16),
            jax.ShapeDtypeStruct(w_out.shape, BF16),
        ),
        in_specs=[anywhere] * 5,
        out_specs=[anywhere] * 4,
        scratch_shapes=[
            vmem((2, 512, 512), BF16),
            vmem((2, 512, 512), BF16),
            vmem((16, 512), BF16),
            vmem((1, 4096, 256), BF16),
            vmem((1, 256, 4096), BF16),
            vmem((2, 512, 512), BF16),
            vmem((16, 512), F32),
            vmem((1, 4096, 256), BF16),
            vmem((1, 256, 4096), BF16),
            vmem((8, 16, LANE), F32),
            vmem((8, 16, LANE), F32),
            vmem((8, 16, LANE), F32),
            vmem((512, LANE), F32),
            vmem((512, LANE), BF16),
            vmem((512, LANE), BF16),
            vmem((16, LANE), F32),
            vmem((16, LANE), BF16),
            vmem((64, 1024), BF16),
            vmem((24, 4096), F32),
            vmem((16, 4096), BF16),
            vmem((32, 16, LANE), BF16),
            vmem((16, LANE), BF16),
            vmem((LANE, 512), BF16),
            vmem((32, LANE), F32),
            vmem((32, LANE), F32),
            vmem((8, 32, LANE), F32),
            vmem((8, 32, LANE), F32),
            vmem((8, 16, LANE), BF16),
            vmem((8, 8, LANE), F32),
            vmem((32, 8, LANE), F32),
            vmem((8, 8, LANE), F32),
            pltpu.SemaphoreType.DMA((5,)),
            pltpu.SemaphoreType.DMA((4,)),
            pltpu.SemaphoreType.DMA((10,)),
            pltpu.SemaphoreType.DMA((10,)),
        ],
        compiler_params=pltpu.CompilerParams(
            collective_id=0, has_side_effects=True, vmem_limit_bytes=48 * 1024 * 1024
        ),
        cost_estimate=pl.CostEstimate(
            flops=400_000_000, bytes_accessed=12_000_000, transcendentals=100_000
        ),
    )(patches, grad_out, phi_t, w_in, w_out)


def solution(mesh):
    in_specs = (
        P(None, "seq", "exp"),
        P(None, "seq", "exp"),
        P(None, "exp"),
        P("exp", None, "seq"),
        P("exp", "seq", None),
    )
    out_specs = (
        P(None, "seq", "exp"),
        P(None, "exp"),
        P("exp", None, "seq"),
        P("exp", "seq", None),
    )
    return jax.shard_map(local, mesh=mesh, in_specs=in_specs, out_specs=out_specs, check_vma=False)
```

```python
import math

import jax
import jax.numpy as jnp
from jax import lax
from jax.experimental import pallas as pl
from jax.experimental.pallas import tpu as pltpu
from jax.sharding import PartitionSpec as P

MESH = pl.DeviceIdType.MESH
F32 = jnp.float32
BF16 = jnp.bfloat16

slope_coef = 0.7978845608
cubic_coef = 0.044715

NS = 32
NZ = 8
LANE = 128


def nn(a, b):
    return lax.dot_general(a, b, (((1,), (0,)), ((), ())), preferred_element_type=F32)


def nt(a, b):
    return lax.dot_general(a, b, (((1,), (1,)), ((), ())), preferred_element_type=F32)


def tn(a, b):
    return lax.dot_general(a, b, (((0,), (0,)), ((), ())), preferred_element_type=F32)


def iota(shape, dim):
    return lax.broadcasted_iota(jnp.int32, shape, dim)


def thirds(value):
    first = value.astype(BF16).astype(F32)
    second = (value - first).astype(BF16).astype(F32)
    return first, second, value - first - second


def spread(column):
    first, second, third = thirds(column)
    lane = iota((8, LANE), 1)
    return jnp.where(
        lane == 0, first, jnp.where(lane == 1, second, jnp.where(lane == 2, third, 0.0))
    )


def kernel(
    patches, grad_out, phi_t, w_in, w_out,
    grad_patches, grad_phi, grad_w_in, grad_w_out,
    pv, gv, phv, wiv, wov, gpv, gphv, gwiv, gwov,
    asend, arecv, logit, cfull, csend, crecv, dtmp, dsend, drecv, rows_f,
    esend, erecv, fsend, frecv, lse_b, dots_b, gsend, grecv, hbuf, isend, irecv, jbuf,
    in_sem, out_sem, send_sem, recv_sem,
):
    r = lax.axis_index("seq")
    z = lax.axis_index("exp")
    source, q = r // 4, lax.rem(r, 4)

    loads = [
        pltpu.make_async_copy(src, dst, in_sem.at[k])
        for k, (src, dst) in enumerate(
            [(phi_t, phv), (patches, pv), (grad_out, gv), (w_in, wiv), (w_out, wov)]
        )
    ]
    for load in loads:
        load.start()

    barrier = pltpu.get_barrier_semaphore()

    def greet(rr, zz):
        pl.semaphore_signal(barrier, inc=1, device_id=(rr, zz), device_id_type=MESH)

    @pl.loop(1, NZ, unroll=True)
    def _(k):
        greet(r, lax.rem(z + k, NZ))

    @pl.loop(1, NS, unroll=True)
    def _(k):
        greet(lax.rem(r + k, NS), z)

    @pl.when(source != z)
    def _():
        @pl.loop(1, NS, unroll=True)
        def _(k):
            greet(lax.rem(r + k, NS), source)

    def remote(src, dst, phase, rr, zz):
        return pltpu.make_async_remote_copy(
            src_ref=src,
            dst_ref=dst,
            send_sem=send_sem.at[phase],
            recv_sem=recv_sem.at[phase],
            device_id=(rr, zz),
            device_id_type=MESH,
        )

    def arrived(ref, phase):
        pltpu.make_async_copy(ref, ref, recv_sem.at[phase]).wait()

    dwait = fwait = csend.at[pl.ds(0, 16 * (NS - 1))]

    def sent(ref, phase):
        pltpu.make_async_copy(ref, ref, send_sem.at[phase]).wait()

    def scatter(piece, place, phase):
        @pl.loop(0, NS, unroll=True)
        def _(k):
            e, qq = lax.rem(z + 1 + k // 4, NZ), lax.rem(r + k, 4)
            rr = z * 4 + qq

            @pl.when((rr != r) | (e != z))
            def _():
                remote(piece(qq, e), place, phase, rr, e).start()

            @pl.when((rr == r) & (e == z))
            def _():
                pltpu.make_async_copy(piece(qq, e), place, recv_sem.at[phase]).start()

    loads[0].wait()
    loads[1].wait()
    phi = phv[...]
    for i in range(2):
        part = nt(phi, pv[i])
        for b in range(4):
            asend[i * 4 + b] = part[:, b * LANE : (b + 1) * LANE]

    extra = jnp.where(source == z, 3 * (NZ - 1), 4 * (NZ - 1))
    pl.semaphore_wait(barrier, NZ - 1 + NS - 1 + extra)

    @pl.loop(1, NZ, unroll=True)
    def _(k):
        zz = lax.rem(z + k, NZ)
        remote(asend.at[zz], arecv.at[z], 0, r, zz).start()

    arecv[z] = asend[z]
    arrived(arecv.at[pl.ds(0, NZ - 1)], 0)
    total = arecv[0]
    for k in range(1, NZ):
        total = total + arecv[k]
    logit[z] = total

    @pl.loop(1, NZ, unroll=True)
    def _(k):
        zz = lax.rem(z + k, NZ)
        remote(logit.at[z], logit.at[z], 1, r, zz).start()

    arrived(logit.at[pl.ds(0, NZ - 1)], 1)
    loads[2].wait()

    diag = iota((32, LANE), 0) == iota((32, LANE), 1)
    peaks, sums = [], []
    for i in range(2):
        li = jnp.concatenate([logit[i * 4 + b] for b in range(4)], axis=1)
        peak = jnp.max(li, axis=1, keepdims=True).astype(BF16).astype(F32)
        e = jnp.exp(li - peak)
        peaks.append(peak)
        sums.append(jnp.sum(e, axis=1, keepdims=True))
        hi = e.astype(BF16)
        lo = (e - hi.astype(F32)).astype(BF16)
        both = nn(jnp.concatenate([hi, lo], axis=0), pv[i])
        slot_part = both[:16] + both[16:]
        ec = jnp.exp(li - jnp.max(li, axis=0, keepdims=True))
        combine_b = (ec / jnp.sum(ec, axis=0, keepdims=True)).astype(BF16)
        grad_part = nn(combine_b, gv[i])
        for half in range(2):
            for c in range(4):
                base = (i * 16 + half * 8) * 16 + c
                rows = slice(half * 8, half * 8 + 8)
                lanes = slice(c * LANE, (c + 1) * LANE)
                high = slot_part[rows, lanes].astype(BF16).astype(F32)
                cfull[pl.ds(base, 8, stride=16), :] = high
                cfull[pl.ds(base + 4, 8, stride=16), :] = slot_part[rows, lanes] - high
                cfull[pl.ds(base + 8, 8, stride=16), :] = grad_part[rows, lanes]
    peak_col = jnp.concatenate(peaks, axis=0)
    sum_col = jnp.concatenate(sums, axis=0)
    peak_row = jnp.sum(jnp.where(diag, peak_col, 0.0), axis=0, keepdims=True)
    sum_row = jnp.sum(jnp.where(diag, sum_col, 0.0), axis=0, keepdims=True)
    stats = (peak_row,) + thirds(sum_row)
    for k, row in enumerate(stats):
        cfull[pl.ds(12 + k, 32, stride=16), :] = jnp.broadcast_to(row, (32, LANE))
    csend[...] = cfull[...].astype(BF16)

    def piece(qq, e):
        row = (qq // 2) * 16 + e * 2 + lax.rem(qq, 2)
        return csend.at[pl.ds(pl.multiple_of(row * 16, 16), 16)]

    scatter(piece, crecv.at[pl.ds(pl.multiple_of(r * 16, 16), 16)], 2)
    arrived(crecv, 2)
    cfull[...] = crecv[...].astype(F32)
    peak_all = cfull[pl.ds(12, 32, stride=16), :]
    sum_all = (
        cfull[pl.ds(13, 32, stride=16), :]
        + cfull[pl.ds(14, 32, stride=16), :]
        + cfull[pl.ds(15, 32, stride=16), :]
    )
    top = jnp.max(peak_all, axis=0, keepdims=True)
    scale = jnp.exp(peak_all - top)
    denom = jnp.sum(scale * sum_all, axis=0, keepdims=True)
    lse_row = top + jnp.log(denom)
    lse_col = jnp.sum(jnp.where(diag, lse_row, 0.0), axis=1, keepdims=True)
    lse_b[...] = jnp.broadcast_to(lse_col, (32, LANE))
    mine = (q // 2) * 16 + z * 2 + lax.rem(q, 2)
    weight = jnp.sum(
        jnp.where(iota((32, LANE), 1) == mine, scale / denom, 0.0), axis=1, keepdims=True
    )
    dtmp[...] = jnp.zeros((16, LANE), F32)
    for c in range(4):
        part = cfull[pl.ds(c, 32, stride=16), :] + cfull[pl.ds(4 + c, 32, stride=16), :]
        row = jnp.sum(weight * part, axis=0, keepdims=True)
        high = row.astype(BF16).astype(F32)
        dtmp[c : c + 1, :] = high
        dtmp[4 + c : 5 + c, :] = row - high
        dtmp[8 + c : 9 + c, :] = jnp.sum(
            cfull[pl.ds(8 + c, 32, stride=16), :], axis=0, keepdims=True
        )
    dsend[...] = dtmp[...].astype(BF16)

    drows = pl.ds(pl.multiple_of(q * 16, 16), 16)
    dlanes = pl.ds(pl.multiple_of(source * LANE, LANE), LANE)

    @pl.loop(1, NS, unroll=True)
    def _(k):
        remote(dsend, drecv.at[drows, dlanes], 3, lax.rem(r + k, NS), z).start()

    drecv[drows, dlanes] = dsend[...]

    at = iota((96, 64), 0)
    c_of, j = at // 24, lax.rem(at, 24)
    part_of = jnp.where(j < 8, 0, jnp.where(j < 16, 8, 4))
    want = lax.rem(j, 4) * 16 + part_of + c_of
    pick = jnp.where(iota((96, 64), 1) == want, 1.0, 0.0).astype(BF16)

    arrived(dwait, 3)
    picked = nn(pick, drecv[...])
    for c in range(4):
        for b in range(NZ):
            rows_f[:, (b * 4 + c) * LANE : (b * 4 + c + 1) * LANE] = picked[
                c * 24 : c * 24 + 24, b * LANE : (b + 1) * LANE
            ]
    loads[3].wait()
    loads[4].wait()
    lhs = rows_f[0:16, :].astype(BF16)
    hidden = nn(lhs, wiv[0])[0:8]
    act_grad = nt(lhs, wov[0])[8:16]
    inner = slope_coef * (hidden + cubic_coef * hidden * hidden * hidden)
    tangent = jnp.tanh(inner)
    active = 0.5 * hidden * (1.0 + tangent)
    slope = 0.5 * (1.0 + tangent) + 0.5 * hidden * (1.0 - tangent * tangent) * slope_coef * (
        1.0 + 3.0 * cubic_coef * hidden * hidden
    )
    pre = act_grad * slope
    upper = iota((8, 256), 0) < 4
    none = jnp.zeros((8, 256), F32)
    active = jnp.where(upper, active, 0.0)
    pre = jnp.where(upper, 0.0, pre)
    active_lo = jnp.concatenate([active, none], axis=0).astype(BF16)
    active_hi = jnp.concatenate([none, active], axis=0).astype(BF16)
    pre_lo = jnp.concatenate([pre, none], axis=0).astype(BF16)
    result = (nn(active_lo, wov[0]) + nt(pre_lo, wiv[0]))[0:8]
    wide = iota((8, 4096), 0) < 4
    dots = jnp.sum(result * (rows_f[0:8, :] + rows_f[16:24, :]), axis=1, keepdims=True)
    high = result.astype(BF16).astype(F32)
    rest = pltpu.roll(result - high, 4, 0)
    esend[...] = jnp.concatenate(
        [high, jnp.where(wide, rest, jnp.concatenate([spread(dots)] * 32, axis=1))], axis=0
    ).astype(BF16)

    def block(qq, e):
        return esend.at[:, pl.ds(pl.multiple_of((e * 4 + qq) * LANE, LANE), LANE)]

    scatter(block, erecv.at[r], 4)

    gwov[0] = tn(active_hi, lhs).astype(BF16)
    gwiv[0] = tn(lhs, pre_lo).astype(BF16)
    stores = [
        pltpu.make_async_copy(gwiv, grad_w_in, out_sem.at[0]),
        pltpu.make_async_copy(gwov, grad_w_out, out_sem.at[1]),
    ]
    for store in stores:
        store.start()

    arrived(erecv, 4)
    total = erecv[0].astype(F32)
    for k in range(1, NS):
        total = total + erecv[k].astype(F32)
    lower = iota((8, LANE), 0) < 4
    rest = pltpu.roll(total[8:16], 4, 0)
    dots = spread(jnp.sum(rest, axis=1, keepdims=True))
    fsend[...] = jnp.concatenate(
        [jnp.where(lower, total[0:8], total[0:8] + rest), jnp.where(lower, dots, 0.0)], axis=0
    ).astype(BF16)

    frows = pl.ds(pl.multiple_of(source * 16, 16), 16)
    flanes = pl.ds(pl.multiple_of(q * LANE, LANE), LANE)

    @pl.loop(1, NS, unroll=True)
    def _(k):
        remote(fsend, frecv.at[frows, flanes], 5, lax.rem(r + k, NS), z).start()

    frecv[frows, flanes] = fsend[...]

    at = iota((96, LANE), 0)
    kind, slot = at // 32, lax.rem(at, 16)
    want = (slot // 2) * 16 + kind * 4 + (lax.rem(at, 32) // 16) * 2 + lax.rem(slot, 2)
    col = iota((96, LANE), 1)
    pick = jnp.where(col == want, 1.0, 0.0).astype(BF16)

    arrived(fwait, 5)
    picked = nn(pick, frecv[...])
    slot_out = picked[0:32].astype(BF16)
    input_grad = picked[32:64].astype(BF16)
    dots_b[...] = jnp.broadcast_to(jnp.sum(picked[64:96, 0:LANE], axis=1, keepdims=True), (32, LANE))
    for i in range(2):
        rows = slice(i * 16, i * 16 + 16)
        comb_part = nt(slot_out[rows], gv[i])
        disp_part = nt(input_grad[rows], pv[i])
        for b in range(4):
            lanes = slice(b * LANE, (b + 1) * LANE)
            gsend[i * 4 + b, 0:16] = comb_part[:, lanes]
            gsend[i * 4 + b, 16:32] = disp_part[:, lanes]

    @pl.loop(1, NZ, unroll=True)
    def _(k):
        zz = lax.rem(z + k, NZ)
        remote(gsend.at[zz], grecv.at[z], 6, r, zz).start()

    grecv[z] = gsend[z]
    chunk = logit[z]
    ec = jnp.exp(chunk - jnp.max(chunk, axis=0, keepdims=True))
    combine = ec / jnp.sum(ec, axis=0, keepdims=True)
    image = pl.ds(pl.multiple_of((z // 4) * 16, 16), 16)
    dispatch = jnp.exp(chunk - lse_b[image, :])
    col_dots = dots_b[image, :]
    arrived(grecv.at[pl.ds(0, NZ - 1)], 6)
    total = grecv[0]
    for k in range(1, NZ):
        total = total + grecv[k]
    comb_grad, disp_grad = total[0:16], total[16:32]
    row_dots = jnp.sum(combine * comb_grad, axis=0, keepdims=True)
    hbuf[z] = (combine * (comb_grad - row_dots) + dispatch * (disp_grad - col_dots)).astype(BF16)

    @pl.loop(1, NZ, unroll=True)
    def _(k):
        zz = lax.rem(z + k, NZ)
        remote(hbuf.at[z], hbuf.at[z], 7, r, zz).start()

    dispatch_b = []
    for i in range(2):
        li = jnp.concatenate([logit[i * 4 + b] for b in range(4)], axis=1)
        dispatch_b.append(jnp.exp(li - lse_col[i * 16 : i * 16 + 16]).astype(BF16))
    arrived(hbuf.at[pl.ds(0, NZ - 1)], 7)
    logit_b = [
        jnp.concatenate([hbuf[i * 4 + b] for b in range(4)], axis=1) for i in range(2)
    ]
    phi_part = nn(logit_b[0], pv[0]) + nn(logit_b[1], pv[1])
    for u in range(8):
        half, c = u // 4, u % 4
        isend[u] = phi_part[half * 8 : half * 8 + 8, c * LANE : (c + 1) * LANE]

    @pl.loop(0, 8, unroll=True)
    def _(u):
        @pl.when(4 * u != r)
        def _():
            remote(isend.at[u], irecv.at[r], 8, 4 * u, z).start()

    for i in range(2):
        left = jnp.concatenate([dispatch_b[i], logit_b[i]], axis=0)
        right = jnp.concatenate([input_grad[i * 16 : i * 16 + 16], phi], axis=0)
        gpv[i] = tn(left, right).astype(BF16)
    stores.append(pltpu.make_async_copy(gpv, grad_patches, out_sem.at[2]))
    stores[2].start()

    tile = r // 4

    @pl.when(lax.rem(r, 4) == 0)
    def _():
        irecv[r] = isend[tile]
        arrived(irecv.at[pl.ds(0, NS - 1)], 8)
        total = irecv[0]
        for k in range(1, NS):
            total = total + irecv[k]
        jbuf[tile] = total * (1.0 / math.sqrt(2 * 512 * NS))

        @pl.loop(1, NS, unroll=True)
        def _(k):
            remote(jbuf.at[tile], jbuf.at[tile], 9, lax.rem(r + k, NS), z).start()

        arrived(jbuf.at[pl.ds(0, 7)], 9)
        sent(irecv.at[pl.ds(0, NS - 1)], 9)
        sent(isend.at[pl.ds(0, 7)], 8)

    @pl.when(lax.rem(r, 4) != 0)
    def _():
        arrived(jbuf, 9)
        sent(isend, 8)

    for u in range(8):
        half, c = u // 4, u % 4
        gphv[half * 8 : half * 8 + 8, c * LANE : (c + 1) * LANE] = jbuf[u]
    stores.append(pltpu.make_async_copy(gphv, grad_phi, out_sem.at[3]))
    stores[3].start()

    sent(asend.at[pl.ds(0, NZ - 1)], 0)
    sent(logit.at[pl.ds(0, NZ - 1)], 1)
    sent(dwait, 3)
    sent(fwait, 5)
    sent(gsend.at[pl.ds(0, NZ - 1)], 6)
    sent(hbuf.at[pl.ds(0, NZ - 1)], 7)

    @pl.when(source == z)
    def _():
        sent(crecv.at[pl.ds(0, 16 * (NS - 1))], 2)
        sent(erecv.at[pl.ds(0, NS - 1)], 4)

    @pl.when(source != z)
    def _():
        sent(crecv, 2)
        sent(erecv, 4)

    for store in stores:
        store.wait()


def store_kernel(gp, gphi, gwi, gwo, gp_out, gphi_out, gwi_out, gwo_out, sem):
    pieces = [(gphi, gphi_out)]
    for k in range(4):
        rows = pl.ds(k * 1024, 1024)
        pieces.append((gwi.at[:, rows], gwi_out.at[:, rows]))
        rows = pl.ds(k * 64, 64)
        pieces.append((gwo.at[:, rows], gwo_out.at[:, rows]))
    for k in range(2):
        pieces.append((gp.at[k], gp_out.at[k]))
    copies = [
        pltpu.make_async_copy(src, dst, sem.at[k]) for k, (src, dst) in enumerate(pieces)
    ]
    for copy in copies:
        copy.start()
    for copy in copies:
        copy.wait()


def local(patches, grad_out, phi_t, w_in, w_out):
    anywhere = pl.BlockSpec(memory_space=pl.ANY)
    hbm = pl.BlockSpec(memory_space=pltpu.HBM)

    def held(arrays, space):
        return [pltpu.with_memory_space_constraint(a, space) for a in arrays]

    vmem = pltpu.VMEM
    shapes = (
        jax.ShapeDtypeStruct(patches.shape, BF16),
        jax.ShapeDtypeStruct(phi_t.shape, F32),
        jax.ShapeDtypeStruct(w_in.shape, BF16),
        jax.ShapeDtypeStruct(w_out.shape, BF16),
    )
    results = pl.pallas_call(
        kernel,
        out_shape=shapes,
        in_specs=[hbm] * 5,
        out_specs=[anywhere] * 4,
        scratch_shapes=[
            vmem((2, 512, 512), BF16),
            vmem((2, 512, 512), BF16),
            vmem((16, 512), BF16),
            vmem((1, 4096, 256), BF16),
            vmem((1, 256, 4096), BF16),
            vmem((2, 512, 512), BF16),
            vmem((16, 512), F32),
            vmem((1, 4096, 256), BF16),
            vmem((1, 256, 4096), BF16),
            vmem((8, 16, LANE), F32),
            vmem((8, 16, LANE), F32),
            vmem((8, 16, LANE), F32),
            vmem((512, LANE), F32),
            vmem((512, LANE), BF16),
            vmem((512, LANE), BF16),
            vmem((16, LANE), F32),
            vmem((16, LANE), BF16),
            vmem((64, 1024), BF16),
            vmem((24, 4096), F32),
            vmem((16, 4096), BF16),
            vmem((32, 16, LANE), BF16),
            vmem((16, LANE), BF16),
            vmem((LANE, 512), BF16),
            vmem((32, LANE), F32),
            vmem((32, LANE), F32),
            vmem((8, 32, LANE), F32),
            vmem((8, 32, LANE), F32),
            vmem((8, 16, LANE), BF16),
            vmem((8, 8, LANE), F32),
            vmem((32, 8, LANE), F32),
            vmem((8, 8, LANE), F32),
            pltpu.SemaphoreType.DMA((5,)),
            pltpu.SemaphoreType.DMA((4,)),
            pltpu.SemaphoreType.DMA((10,)),
            pltpu.SemaphoreType.DMA((10,)),
        ],
        compiler_params=pltpu.CompilerParams(
            collective_id=0, has_side_effects=True, vmem_limit_bytes=28 * 1024 * 1024
        ),
        cost_estimate=pl.CostEstimate(
            flops=400_000_000, bytes_accessed=12_000_000, transcendentals=100_000
        ),
    )(*held((patches, grad_out, phi_t, w_in, w_out), pltpu.HBM))
    return pl.pallas_call(
        store_kernel,
        out_shape=shapes,
        in_specs=[anywhere] * 4,
        out_specs=[hbm] * 4,
        scratch_shapes=[pltpu.SemaphoreType.DMA((11,))],
        compiler_params=pltpu.CompilerParams(vmem_limit_bytes=4 * 1024 * 1024),
    )(*held(results, pltpu.VMEM))


def solution(mesh):
    in_specs = (
        P(None, "seq", "exp"),
        P(None, "seq", "exp"),
        P(None, "exp"),
        P("exp", None, "seq"),
        P("exp", "seq", None),
    )
    out_specs = (
        P(None, "seq", "exp"),
        P(None, "exp"),
        P("exp", None, "seq"),
        P("exp", "seq", None),
    )
    return jax.shard_map(local, mesh=mesh, in_specs=in_specs, out_specs=out_specs, check_vma=False)
```

```python
import math

import jax
import jax.numpy as jnp
from jax import lax
from jax.experimental import pallas as pl
from jax.experimental.pallas import tpu as pltpu
from jax.sharding import PartitionSpec as P

MESH = pl.DeviceIdType.MESH
F32 = jnp.float32
BF16 = jnp.bfloat16

slope_coef = 0.7978845608
cubic_coef = 0.044715

NS = 32
NZ = 8
LANE = 128


def ring(d, n):
    return min(d, n - d)


ALONG_EXP = sorted(range(1, NZ), key=lambda d: -ring(d, NZ))
CHIPS = sorted(
    ((dy, dx) for dy in range(4) for dx in range(4)), key=lambda d: -ring(d[0], 4) - ring(d[1], 4)
)
ALONG_SEQ = [(dy, dx, dc) for dy, dx in CHIPS for dc in range(2) if (dy, dx, dc) != (0, 0, 0)]


def nn(a, b):
    return lax.dot_general(a, b, (((1,), (0,)), ((), ())), preferred_element_type=F32)


def nt(a, b):
    return lax.dot_general(a, b, (((1,), (1,)), ((), ())), preferred_element_type=F32)


def tn(a, b):
    return lax.dot_general(a, b, (((0,), (0,)), ((), ())), preferred_element_type=F32)


def iota(shape, dim):
    return lax.broadcasted_iota(jnp.int32, shape, dim)


def thirds(value):
    first = value.astype(BF16).astype(F32)
    second = (value - first).astype(BF16).astype(F32)
    return first, second, value - first - second


def spread(column):
    first, second, third = thirds(column)
    lane = iota((8, LANE), 1)
    return jnp.where(
        lane == 0, first, jnp.where(lane == 1, second, jnp.where(lane == 2, third, 0.0))
    )


def kernel(
    patches, grad_out, phi_t, w_in, w_out,
    grad_patches, grad_phi, grad_w_in, grad_w_out,
    pv, gv, phv, wiv, wov,
    asend, arecv, logit, cfull, csend, crecv, dtmp, dsend, drecv, rows_f,
    esend, erecv, fsend, frecv, lse_b, dots_b, gsend, grecv, hbuf, pair, paired, isend, irecv, halves,
    in_sem, send_sem, recv_sem,
):
    r = lax.axis_index("seq")
    z = lax.axis_index("exp")
    source, q = r // 4, lax.rem(r, 4)

    y, x, core = r // 8, lax.rem(r // 2, 4), lax.rem(r, 2)

    def at_offset(dy, dx, dc):
        return (lax.rem(y + dy, 4) * 4 + lax.rem(x + dx, 4)) * 2 + lax.rem(core + dc, 2)

    loads = [
        pltpu.make_async_copy(src, dst, in_sem.at[k])
        for k, (src, dst) in enumerate(
            [(phi_t, phv), (patches, pv), (grad_out, gv), (w_in, wiv), (w_out, wov)]
        )
    ]
    for load in loads:
        load.start()

    barrier = pltpu.get_barrier_semaphore()

    def greet(rr, zz):
        pl.semaphore_signal(barrier, inc=1, device_id=(rr, zz), device_id_type=MESH)

    @pl.loop(1, NZ)
    def _(k):
        greet(r, lax.rem(z + k, NZ))

    @pl.loop(1, NS)
    def _(k):
        greet(lax.rem(r + k, NS), z)

    @pl.when(source != z)
    def _():
        @pl.loop(1, NS)
        def _(k):
            greet(lax.rem(r + k, NS), source)

    def remote(src, dst, phase, rr, zz):
        return pltpu.make_async_remote_copy(
            src_ref=src,
            dst_ref=dst,
            send_sem=send_sem.at[phase],
            recv_sem=recv_sem.at[phase],
            device_id=(rr, zz),
            device_id_type=MESH,
        )

    def arrived(ref, phase):
        pltpu.make_async_copy(ref, ref, recv_sem.at[phase]).wait()

    dwait = fwait = csend.at[pl.ds(0, 16 * (NS - 1))]

    def sent(ref, phase):
        pltpu.make_async_copy(ref, ref, send_sem.at[phase]).wait()

    def scatter(piece, place, phase):
        for d in ALONG_EXP:
            e = lax.rem(z + d, NZ)
            for k in range(4):
                qq = lax.rem(r + k, 4)
                remote(piece(qq, e), place, phase, z * 4 + qq, e).start()
        for k in range(4):
            qq = lax.rem(r + k, 4)
            rr = z * 4 + qq

            @pl.when(rr != r)
            def _():
                remote(piece(qq, z), place, phase, rr, z).start()

            @pl.when(rr == r)
            def _():
                pltpu.make_async_copy(piece(qq, z), place, recv_sem.at[phase]).start()

    loads[0].wait()
    loads[1].wait()
    phi = phv[...]
    for i in range(2):
        part = nt(phi, pv[i])
        for b in range(4):
            asend[i * 4 + b] = part[:, b * LANE : (b + 1) * LANE]

    extra = jnp.where(source == z, 3 * (NZ - 1), 4 * (NZ - 1))
    pl.semaphore_wait(barrier, NZ - 1 + NS - 1 + extra)

    for d in ALONG_EXP:
        zz = lax.rem(z + d, NZ)
        remote(asend.at[zz], arecv.at[z], 0, r, zz).start()

    arecv[z] = asend[z]
    arrived(arecv.at[pl.ds(0, NZ - 1)], 0)
    total = arecv[0]
    for k in range(1, NZ):
        total = total + arecv[k]
    logit[z] = total

    for d in ALONG_EXP:
        zz = lax.rem(z + d, NZ)
        remote(logit.at[z], logit.at[z], 1, r, zz).start()

    arrived(logit.at[pl.ds(0, NZ - 1)], 1)
    loads[2].wait()

    diag = iota((32, LANE), 0) == iota((32, LANE), 1)
    peaks, sums = [], []
    for i in range(2):
        li = jnp.concatenate([logit[i * 4 + b] for b in range(4)], axis=1)
        peak = jnp.max(li, axis=1, keepdims=True).astype(BF16).astype(F32)
        e = jnp.exp(li - peak)
        peaks.append(peak)
        sums.append(jnp.sum(e, axis=1, keepdims=True))
        hi = e.astype(BF16)
        lo = (e - hi.astype(F32)).astype(BF16)
        both = nn(jnp.concatenate([hi, lo], axis=0), pv[i])
        slot_part = both[:16] + both[16:]
        ec = jnp.exp(li - jnp.max(li, axis=0, keepdims=True))
        combine_b = (ec / jnp.sum(ec, axis=0, keepdims=True)).astype(BF16)
        grad_part = nn(combine_b, gv[i])
        for half in range(2):
            for c in range(4):
                base = (i * 16 + half * 8) * 16 + c
                rows = slice(half * 8, half * 8 + 8)
                lanes = slice(c * LANE, (c + 1) * LANE)
                high = slot_part[rows, lanes].astype(BF16).astype(F32)
                cfull[pl.ds(base, 8, stride=16), :] = high
                cfull[pl.ds(base + 4, 8, stride=16), :] = slot_part[rows, lanes] - high
                cfull[pl.ds(base + 8, 8, stride=16), :] = grad_part[rows, lanes]
    peak_col = jnp.concatenate(peaks, axis=0)
    sum_col = jnp.concatenate(sums, axis=0)
    peak_row = jnp.sum(jnp.where(diag, peak_col, 0.0), axis=0, keepdims=True)
    sum_row = jnp.sum(jnp.where(diag, sum_col, 0.0), axis=0, keepdims=True)
    stats = (peak_row,) + thirds(sum_row)
    for k, row in enumerate(stats):
        cfull[pl.ds(12 + k, 32, stride=16), :] = jnp.broadcast_to(row, (32, LANE))
    csend[...] = cfull[...].astype(BF16)

    def piece(qq, e):
        row = (qq // 2) * 16 + e * 2 + lax.rem(qq, 2)
        return csend.at[pl.ds(pl.multiple_of(row * 16, 16), 16)]

    scatter(piece, crecv.at[pl.ds(pl.multiple_of(r * 16, 16), 16)], 2)
    arrived(crecv, 2)
    cfull[...] = crecv[...].astype(F32)
    peak_all = cfull[pl.ds(12, 32, stride=16), :]
    sum_all = (
        cfull[pl.ds(13, 32, stride=16), :]
        + cfull[pl.ds(14, 32, stride=16), :]
        + cfull[pl.ds(15, 32, stride=16), :]
    )
    top = jnp.max(peak_all, axis=0, keepdims=True)
    scale = jnp.exp(peak_all - top)
    denom = jnp.sum(scale * sum_all, axis=0, keepdims=True)
    lse_row = top + jnp.log(denom)
    lse_col = jnp.sum(jnp.where(diag, lse_row, 0.0), axis=1, keepdims=True)
    lse_b[...] = jnp.broadcast_to(lse_col, (32, LANE))
    mine = (q // 2) * 16 + z * 2 + lax.rem(q, 2)
    weight = jnp.sum(
        jnp.where(iota((32, LANE), 1) == mine, scale / denom, 0.0), axis=1, keepdims=True
    )
    dtmp[...] = jnp.zeros((16, LANE), F32)
    for c in range(4):
        part = cfull[pl.ds(c, 32, stride=16), :] + cfull[pl.ds(4 + c, 32, stride=16), :]
        row = jnp.sum(weight * part, axis=0, keepdims=True)
        high = row.astype(BF16).astype(F32)
        dtmp[c : c + 1, :] = high
        dtmp[4 + c : 5 + c, :] = row - high
        dtmp[8 + c : 9 + c, :] = jnp.sum(
            cfull[pl.ds(8 + c, 32, stride=16), :], axis=0, keepdims=True
        )
    dsend[...] = dtmp[...].astype(BF16)

    drows = pl.ds(pl.multiple_of(q * 16, 16), 16)
    dlanes = pl.ds(pl.multiple_of(source * LANE, LANE), LANE)

    for d in ALONG_SEQ:
        remote(dsend, drecv.at[drows, dlanes], 3, at_offset(*d), z).start()

    drecv[drows, dlanes] = dsend[...]

    at = iota((96, 64), 0)
    c_of, j = at // 24, lax.rem(at, 24)
    part_of = jnp.where(j < 8, 0, jnp.where(j < 16, 8, 4))
    want = lax.rem(j, 4) * 16 + part_of + c_of
    pick = jnp.where(iota((96, 64), 1) == want, 1.0, 0.0).astype(BF16)

    arrived(dwait, 3)
    picked = nn(pick, drecv[...])
    for c in range(4):
        for b in range(NZ):
            rows_f[:, (b * 4 + c) * LANE : (b * 4 + c + 1) * LANE] = picked[
                c * 24 : c * 24 + 24, b * LANE : (b + 1) * LANE
            ]
    loads[3].wait()
    loads[4].wait()
    lhs = rows_f[0:16, :].astype(BF16)
    hidden = nn(lhs, wiv[0])[0:8]
    act_grad = nt(lhs, wov[0])[8:16]
    inner = slope_coef * (hidden + cubic_coef * hidden * hidden * hidden)
    tangent = jnp.tanh(inner)
    active = 0.5 * hidden * (1.0 + tangent)
    slope = 0.5 * (1.0 + tangent) + 0.5 * hidden * (1.0 - tangent * tangent) * slope_coef * (
        1.0 + 3.0 * cubic_coef * hidden * hidden
    )
    pre = act_grad * slope
    upper = iota((8, 256), 0) < 4
    none = jnp.zeros((8, 256), F32)
    active = jnp.where(upper, active, 0.0)
    pre = jnp.where(upper, 0.0, pre)
    active_lo = jnp.concatenate([active, none], axis=0).astype(BF16)
    active_hi = jnp.concatenate([none, active], axis=0).astype(BF16)
    pre_lo = jnp.concatenate([pre, none], axis=0).astype(BF16)
    result = (nn(active_lo, wov[0]) + nt(pre_lo, wiv[0]))[0:8]
    wide = iota((8, 4096), 0) < 4
    dots = jnp.sum(result * (rows_f[0:8, :] + rows_f[16:24, :]), axis=1, keepdims=True)
    high = result.astype(BF16).astype(F32)
    rest = pltpu.roll(result - high, 4, 0)
    esend[...] = jnp.concatenate(
        [high, jnp.where(wide, rest, jnp.concatenate([spread(dots)] * 32, axis=1))], axis=0
    ).astype(BF16)

    def block(qq, e):
        return esend.at[:, pl.ds(pl.multiple_of((e * 4 + qq) * LANE, LANE), LANE)]

    scatter(block, erecv.at[r], 4)

    grad_w_out[0] = tn(active_hi, lhs).astype(BF16)
    grad_w_in[0] = tn(lhs, pre_lo).astype(BF16)

    arrived(erecv, 4)
    total = erecv[0].astype(F32)
    for k in range(1, NS):
        total = total + erecv[k].astype(F32)
    lower = iota((8, LANE), 0) < 4
    rest = pltpu.roll(total[8:16], 4, 0)
    dots = spread(jnp.sum(rest, axis=1, keepdims=True))
    fsend[...] = jnp.concatenate(
        [jnp.where(lower, total[0:8], total[0:8] + rest), jnp.where(lower, dots, 0.0)], axis=0
    ).astype(BF16)

    frows = pl.ds(pl.multiple_of(source * 16, 16), 16)
    flanes = pl.ds(pl.multiple_of(q * LANE, LANE), LANE)

    for d in ALONG_SEQ:
        remote(fsend, frecv.at[frows, flanes], 5, at_offset(*d), z).start()

    frecv[frows, flanes] = fsend[...]

    at = iota((96, LANE), 0)
    kind, slot = at // 32, lax.rem(at, 16)
    want = (slot // 2) * 16 + kind * 4 + (lax.rem(at, 32) // 16) * 2 + lax.rem(slot, 2)
    col = iota((96, LANE), 1)
    pick = jnp.where(col == want, 1.0, 0.0).astype(BF16)

    arrived(fwait, 5)
    picked = nn(pick, frecv[...])
    slot_out = picked[0:32].astype(BF16)
    input_grad = picked[32:64].astype(BF16)
    dots_b[...] = jnp.broadcast_to(jnp.sum(picked[64:96, 0:LANE], axis=1, keepdims=True), (32, LANE))
    for i in range(2):
        rows = slice(i * 16, i * 16 + 16)
        comb_part = nt(slot_out[rows], gv[i])
        disp_part = nt(input_grad[rows], pv[i])
        for b in range(4):
            lanes = slice(b * LANE, (b + 1) * LANE)
            gsend[i * 4 + b, 0:16] = comb_part[:, lanes].astype(BF16)
            gsend[i * 4 + b, 16:32] = disp_part[:, lanes].astype(BF16)

    for d in ALONG_EXP:
        zz = lax.rem(z + d, NZ)
        remote(gsend.at[zz], grecv.at[z], 6, r, zz).start()

    grecv[z] = gsend[z]
    chunk = logit[z]
    ec = jnp.exp(chunk - jnp.max(chunk, axis=0, keepdims=True))
    combine = ec / jnp.sum(ec, axis=0, keepdims=True)
    image = pl.ds(pl.multiple_of((z // 4) * 16, 16), 16)
    dispatch = jnp.exp(chunk - lse_b[image, :])
    col_dots = dots_b[image, :]
    arrived(grecv.at[pl.ds(0, NZ - 1)], 6)
    total = grecv[0].astype(F32)
    for k in range(1, NZ):
        total = total + grecv[k].astype(F32)
    comb_grad, disp_grad = total[0:16], total[16:32]
    row_dots = jnp.sum(combine * comb_grad, axis=0, keepdims=True)
    hbuf[z] = (combine * (comb_grad - row_dots) + dispatch * (disp_grad - col_dots)).astype(BF16)

    for d in ALONG_EXP:
        zz = lax.rem(z + d, NZ)
        remote(hbuf.at[z], hbuf.at[z], 7, r, zz).start()

    dispatch_b = []
    for i in range(2):
        li = jnp.concatenate([logit[i * 4 + b] for b in range(4)], axis=1)
        dispatch_b.append(jnp.exp(li - lse_col[i * 16 : i * 16 + 16]).astype(BF16))
    arrived(hbuf.at[pl.ds(0, NZ - 1)], 7)
    logit_b = [
        jnp.concatenate([hbuf[i * 4 + b] for b in range(4)], axis=1) for i in range(2)
    ]
    phi_part = nn(logit_b[0], pv[0]) + nn(logit_b[1], pv[1])
    for h in range(2):
        slots = slice(h * 8, h * 8 + 8)
        pair[h] = jnp.concatenate([phi_part[slots, 0:256], phi_part[slots, 256:512]], axis=0)

    def spread_patches(i):
        left = jnp.concatenate([dispatch_b[i], logit_b[i]], axis=0)
        right = jnp.concatenate([input_grad[i * 16 : i * 16 + 16], phi], axis=0)
        grad_patches[i] = tn(left, right).astype(BF16)

    sibling = at_offset(0, 0, 1)
    trade = remote(pair.at[1 - core], paired, 8, sibling, z)
    trade.start()
    spread_patches(0)
    trade.wait_recv()
    half_sum = pair[core] + paired[...]
    isend[...] = half_sum.astype(BF16)
    for dy, dx in CHIPS[:-1]:
        remote(isend, irecv.at[r // 2], 9, at_offset(dy, dx, 0), z).start()
    irecv[r // 2] = isend[...]
    spread_patches(1)
    arrived(irecv.at[pl.ds(0, 15)], 9)
    total = irecv[0].astype(F32)
    for k in range(1, 16):
        total = total + irecv[k].astype(F32)
    halves[core] = total * (1.0 / math.sqrt(2 * 512 * NS))
    back = remote(halves.at[core], halves.at[core], 10, sibling, z)
    back.start()
    sent(asend.at[pl.ds(0, NZ - 1)], 0)
    sent(logit.at[pl.ds(0, NZ - 1)], 1)
    sent(dwait, 3)
    sent(fwait, 5)
    sent(gsend.at[pl.ds(0, NZ - 1)], 6)
    sent(hbuf.at[pl.ds(0, NZ - 1)], 7)
    trade.wait_send()
    sent(irecv.at[pl.ds(0, 15)], 9)

    @pl.when(source == z)
    def _():
        sent(crecv.at[pl.ds(0, 16 * (NS - 1))], 2)
        sent(erecv.at[pl.ds(0, NS - 1)], 4)

    @pl.when(source != z)
    def _():
        sent(crecv, 2)
        sent(erecv, 4)

    back.wait()
    for h in range(2):
        grad_phi[h * 8 : h * 8 + 8, 0:256] = halves[h, 0:8]
        grad_phi[h * 8 : h * 8 + 8, 256:512] = halves[h, 8:16]


def store_kernel(gp, gphi, gwi, gwo, gp_out, gphi_out, gwi_out, gwo_out, sem):
    pieces = [(gphi, gphi_out)]
    for k in range(4):
        rows = pl.ds(k * 1024, 1024)
        pieces.append((gwi.at[:, rows], gwi_out.at[:, rows]))
        rows = pl.ds(k * 64, 64)
        pieces.append((gwo.at[:, rows], gwo_out.at[:, rows]))
    for k in range(2):
        pieces.append((gp.at[k], gp_out.at[k]))
    copies = [
        pltpu.make_async_copy(src, dst, sem.at[k]) for k, (src, dst) in enumerate(pieces)
    ]
    for copy in copies:
        copy.start()
    for copy in copies:
        copy.wait()


def local(patches, grad_out, phi_t, w_in, w_out):
    anywhere = pl.BlockSpec(memory_space=pl.ANY)
    hbm = pl.BlockSpec(memory_space=pltpu.HBM)

    def held(arrays, space):
        return [pltpu.with_memory_space_constraint(a, space) for a in arrays]

    vmem = pltpu.VMEM
    shapes = (
        jax.ShapeDtypeStruct(patches.shape, BF16),
        jax.ShapeDtypeStruct(phi_t.shape, F32),
        jax.ShapeDtypeStruct(w_in.shape, BF16),
        jax.ShapeDtypeStruct(w_out.shape, BF16),
    )
    results = pl.pallas_call(
        kernel,
        out_shape=shapes,
        in_specs=[hbm] * 5,
        out_specs=[pl.BlockSpec(memory_space=pltpu.VMEM)] * 4,
        scratch_shapes=[
            vmem((2, 512, 512), BF16),
            vmem((2, 512, 512), BF16),
            vmem((16, 512), BF16),
            vmem((1, 4096, 256), BF16),
            vmem((1, 256, 4096), BF16),
            vmem((8, 16, LANE), F32),
            vmem((8, 16, LANE), F32),
            vmem((8, 16, LANE), F32),
            vmem((512, LANE), F32),
            vmem((512, LANE), BF16),
            vmem((512, LANE), BF16),
            vmem((16, LANE), F32),
            vmem((16, LANE), BF16),
            vmem((64, 1024), BF16),
            vmem((24, 4096), F32),
            vmem((16, 4096), BF16),
            vmem((32, 16, LANE), BF16),
            vmem((16, LANE), BF16),
            vmem((LANE, 512), BF16),
            vmem((32, LANE), F32),
            vmem((32, LANE), F32),
            vmem((8, 32, LANE), BF16),
            vmem((8, 32, LANE), BF16),
            vmem((8, 16, LANE), BF16),
            vmem((2, 16, 256), F32),
            vmem((16, 256), F32),
            vmem((16, 256), BF16),
            vmem((16, 16, 256), BF16),
            vmem((2, 16, 256), F32),
            pltpu.SemaphoreType.DMA((5,)),
            pltpu.SemaphoreType.DMA((11,)),
            pltpu.SemaphoreType.DMA((11,)),
        ],
        compiler_params=pltpu.CompilerParams(
            collective_id=0, has_side_effects=True, vmem_limit_bytes=28 * 1024 * 1024
        ),
        cost_estimate=pl.CostEstimate(
            flops=400_000_000, bytes_accessed=12_000_000, transcendentals=100_000
        ),
    )(*held((patches, grad_out, phi_t, w_in, w_out), pltpu.HBM))
    return pl.pallas_call(
        store_kernel,
        out_shape=shapes,
        in_specs=[anywhere] * 4,
        out_specs=[hbm] * 4,
        scratch_shapes=[pltpu.SemaphoreType.DMA((11,))],
        compiler_params=pltpu.CompilerParams(vmem_limit_bytes=4 * 1024 * 1024),
    )(*held(results, pltpu.VMEM))


def solution(mesh):
    in_specs = (
        P(None, "seq", "exp"),
        P(None, "seq", "exp"),
        P(None, "exp"),
        P("exp", None, "seq"),
        P("exp", "seq", None),
    )
    out_specs = (
        P(None, "seq", "exp"),
        P(None, "exp"),
        P("exp", None, "seq"),
        P("exp", "seq", None),
    )
    return jax.shard_map(local, mesh=mesh, in_specs=in_specs, out_specs=out_specs, check_vma=False)
```

```python
import math

import jax
import jax.numpy as jnp
from jax import lax
from jax.experimental import pallas as pl
from jax.experimental.pallas import tpu as pltpu
from jax.sharding import PartitionSpec as P

MESH = pl.DeviceIdType.MESH
F32 = jnp.float32
BF16 = jnp.bfloat16

slope_coef = 0.7978845608
cubic_coef = 0.044715

NS = 32
NZ = 8
LANE = 128


def ring(d, n):
    return min(d, n - d)


ALONG_EXP = sorted(range(1, NZ), key=lambda d: -ring(d, NZ))
CHIPS = sorted(
    ((dy, dx) for dy in range(4) for dx in range(4)), key=lambda d: -ring(d[0], 4) - ring(d[1], 4)
)
ALONG_SEQ = [(dy, dx, dc) for dy, dx in CHIPS for dc in range(2) if (dy, dx, dc) != (0, 0, 0)]


def nn(a, b):
    return lax.dot_general(a, b, (((1,), (0,)), ((), ())), preferred_element_type=F32)


def nt(a, b):
    return lax.dot_general(a, b, (((1,), (1,)), ((), ())), preferred_element_type=F32)


def tn(a, b):
    return lax.dot_general(a, b, (((0,), (0,)), ((), ())), preferred_element_type=F32)


def iota(shape, dim):
    return lax.broadcasted_iota(jnp.int32, shape, dim)


def thirds(value):
    first = value.astype(BF16).astype(F32)
    second = (value - first).astype(BF16).astype(F32)
    return first, second, value - first - second


def spread(column):
    first, second, third = thirds(column)
    lane = iota((8, LANE), 1)
    return jnp.where(
        lane == 0, first, jnp.where(lane == 1, second, jnp.where(lane == 2, third, 0.0))
    )


def kernel(
    patches, grad_out, phi_t, w_in, w_out,
    grad_patches, grad_phi, grad_w_in, grad_w_out,
    pv, gv, phv, wiv, wov, pvt, gvt, wit, wot,
    asend, arecv, logit, cfull, csend, crecv, dtmp, dsend, drecv, rows_f,
    esend, erecv, fsend, frecv, lse_b, dots_b, gsend, grecv, hbuf, pair, paired, isend, irecv,
    in_sem, send_sem, recv_sem, d_sem, known,
):
    r = lax.axis_index("seq")
    z = lax.axis_index("exp")
    source, q = r // 4, lax.rem(r, 4)

    y, x, core = r // 8, lax.rem(r // 2, 4), lax.rem(r, 2)

    def at_offset(dy, dx, dc):
        return (lax.rem(y + dy, 4) * 4 + lax.rem(x + dx, 4)) * 2 + lax.rem(core + dc, 2)

    loads = [
        pltpu.make_async_copy(src, dst, in_sem.at[k])
        for k, (src, dst) in enumerate(
            [
                (phi_t, phv), (patches.at[0], pv.at[0]), (patches.at[1], pv.at[1]),
                (grad_out, gv), (w_out, wov), (w_in, wiv),
            ]
        )
    ]
    for load in loads[:3]:
        load.start()

    barrier = pltpu.get_barrier_semaphore()

    def greet(rr, zz):
        pl.semaphore_signal(barrier, inc=1, device_id=(rr, zz), device_id_type=MESH)

    x_line = [at_offset(0, d, 0) for d in (2, 1, 3)]
    y_line = [at_offset(d, 0, 0) for d in (2, 1, 3)]
    sibling = at_offset(0, 0, 1)

    for d in ALONG_EXP:
        greet(r, lax.rem(z + d, NZ))
    for rr in x_line + y_line + [sibling]:
        greet(rr, z)

    def tell(line, step):
        for rr in line:
            pl.semaphore_signal(known.at[step], inc=1, device_id=(rr, z), device_id_type=MESH)

    def remote(src, dst, phase, rr, zz):
        return pltpu.make_async_remote_copy(
            src_ref=src,
            dst_ref=dst,
            send_sem=send_sem.at[phase],
            recv_sem=recv_sem.at[phase],
            device_id=(rr, zz),
            device_id_type=MESH,
        )

    def arrived(ref, phase):
        pltpu.make_async_copy(ref, ref, recv_sem.at[phase]).wait()

    dwait = fwait = csend.at[pl.ds(0, 16 * (NS - 1))]

    def sent(ref, phase):
        pltpu.make_async_copy(ref, ref, send_sem.at[phase]).wait()

    def scatter(piece, place, phase):
        for d in ALONG_EXP:
            e = lax.rem(z + d, NZ)
            for k in range(4):
                qq = lax.rem(r + k, 4)
                remote(piece(qq, e), place, phase, z * 4 + qq, e).start()
        for k in range(4):
            qq = lax.rem(r + k, 4)
            rr = z * 4 + qq

            @pl.when(rr != r)
            def _():
                remote(piece(qq, z), place, phase, rr, z).start()

            @pl.when(rr == r)
            def _():
                pltpu.make_async_copy(piece(qq, z), place, recv_sem.at[phase]).start()

    loads[0].wait()
    phi = phv[...]
    for i in range(2):
        loads[1 + i].wait()
        part = nt(phi, pv[i])
        for b in range(4):
            asend[i * 4 + b] = part[:, b * LANE : (b + 1) * LANE]
    for load in loads[3:]:
        load.start()

    pl.semaphore_wait(barrier, NZ - 1 + 7)

    for d in ALONG_EXP:
        zz = lax.rem(z + d, NZ)
        remote(asend.at[zz], arecv.at[z], 0, r, zz).start()

    arecv[z] = asend[z]
    tell([sibling], 0)
    pl.semaphore_wait(known.at[0], 1)
    tell(x_line, 1)
    loads[4].wait()
    wot[...] = wov[0].T
    arrived(arecv.at[pl.ds(0, NZ - 1)], 0)
    total = arecv[0]
    for k in range(1, NZ):
        total = total + arecv[k]
    logit[z] = total

    for d in ALONG_EXP:
        zz = lax.rem(z + d, NZ)
        remote(logit.at[z], logit.at[z], 1, r, zz).start()

    pl.semaphore_wait(known.at[1], 3)
    tell(y_line, 2)
    loads[5].wait()
    wit[...] = wiv[0].T
    loads[3].wait()
    arrived(logit.at[pl.ds(0, NZ - 1)], 1)
    pl.semaphore_wait(known.at[2], 3)

    diag = iota((32, LANE), 0) == iota((32, LANE), 1)
    peaks, sums = [], []
    for i in range(2):
        li = jnp.concatenate([logit[i * 4 + b] for b in range(4)], axis=1)
        peak = jnp.max(li, axis=1, keepdims=True).astype(BF16).astype(F32)
        e = jnp.exp(li - peak)
        peaks.append(peak)
        sums.append(jnp.sum(e, axis=1, keepdims=True))
        hi = e.astype(BF16)
        lo = (e - hi.astype(F32)).astype(BF16)
        both = nn(jnp.concatenate([hi, lo], axis=0), pv[i])
        slot_part = both[:16] + both[16:]
        ec = jnp.exp(li - jnp.max(li, axis=0, keepdims=True))
        combine_b = (ec / jnp.sum(ec, axis=0, keepdims=True)).astype(BF16)
        grad_part = nn(combine_b, gv[i])
        for half in range(2):
            for c in range(4):
                base = (i * 16 + half * 8) * 16 + c
                rows = slice(half * 8, half * 8 + 8)
                lanes = slice(c * LANE, (c + 1) * LANE)
                high = slot_part[rows, lanes].astype(BF16).astype(F32)
                cfull[pl.ds(base, 8, stride=16), :] = high
                cfull[pl.ds(base + 4, 8, stride=16), :] = slot_part[rows, lanes] - high
                cfull[pl.ds(base + 8, 8, stride=16), :] = grad_part[rows, lanes]
    peak_col = jnp.concatenate(peaks, axis=0)
    sum_col = jnp.concatenate(sums, axis=0)
    peak_row = jnp.sum(jnp.where(diag, peak_col, 0.0), axis=0, keepdims=True)
    sum_row = jnp.sum(jnp.where(diag, sum_col, 0.0), axis=0, keepdims=True)
    stats = (peak_row,) + thirds(sum_row)
    for k, row in enumerate(stats):
        cfull[pl.ds(12 + k, 32, stride=16), :] = jnp.broadcast_to(row, (32, LANE))
    csend[...] = cfull[...].astype(BF16)

    def piece(qq, e):
        row = (qq // 2) * 16 + e * 2 + lax.rem(qq, 2)
        return csend.at[pl.ds(pl.multiple_of(row * 16, 16), 16)]

    scatter(piece, crecv.at[pl.ds(pl.multiple_of(r * 16, 16), 16)], 2)
    for i in range(2):
        pvt[i] = pv[i].T
        gvt[i] = gv[i].T
    arrived(crecv, 2)
    cfull[...] = crecv[...].astype(F32)
    peak_all = cfull[pl.ds(12, 32, stride=16), :]
    sum_all = (
        cfull[pl.ds(13, 32, stride=16), :]
        + cfull[pl.ds(14, 32, stride=16), :]
        + cfull[pl.ds(15, 32, stride=16), :]
    )
    top = jnp.max(peak_all, axis=0, keepdims=True)
    scale = jnp.exp(peak_all - top)
    denom = jnp.sum(scale * sum_all, axis=0, keepdims=True)
    lse_row = top + jnp.log(denom)
    lse_col = jnp.sum(jnp.where(diag, lse_row, 0.0), axis=1, keepdims=True)
    lse_b[...] = jnp.broadcast_to(lse_col, (32, LANE))
    mine = (q // 2) * 16 + z * 2 + lax.rem(q, 2)
    weight = jnp.sum(
        jnp.where(iota((32, LANE), 1) == mine, scale / denom, 0.0), axis=1, keepdims=True
    )
    dtmp[...] = jnp.zeros((16, LANE), F32)
    for c in range(4):
        part = cfull[pl.ds(c, 32, stride=16), :] + cfull[pl.ds(4 + c, 32, stride=16), :]
        row = jnp.sum(weight * part, axis=0, keepdims=True)
        high = row.astype(BF16).astype(F32)
        dtmp[c : c + 1, :] = high
        dtmp[4 + c : 5 + c, :] = row - high
        dtmp[8 + c : 9 + c, :] = jnp.sum(
            cfull[pl.ds(8 + c, 32, stride=16), :], axis=0, keepdims=True
        )
    dsend[...] = dtmp[...].astype(BF16)

    drows = pl.ds(pl.multiple_of(q * 16, 16), 16)
    dlanes = pl.ds(pl.multiple_of(source * LANE, LANE), LANE)

    for dy, dx, dc in ALONG_SEQ:
        pltpu.make_async_remote_copy(
            src_ref=dsend,
            dst_ref=drecv.at[drows, dlanes],
            send_sem=send_sem.at[3],
            recv_sem=d_sem.at[(4 - dy) % 4],
            device_id=(at_offset(dy, dx, dc), z),
            device_id_type=MESH,
        ).start()

    drecv[drows, dlanes] = dsend[...]

    at = iota((96, 64), 0)
    c_of, j = at // 24, lax.rem(at, 24)
    part_of = jnp.where(j < 8, 0, jnp.where(j < 16, 8, 4))
    want = lax.rem(j, 4) * 16 + part_of + c_of
    pick = jnp.where(iota((96, 64), 1) == want, 1.0, 0.0).astype(BF16)

    hidden = act_grad = None
    for g in (0, 1, 3, 2):
        come = csend.at[pl.ds(0, 16 * (7 if g == 0 else 8))]
        pltpu.make_async_copy(come, come, d_sem.at[g]).wait()
        first = lax.rem(y + g, 4) * 2
        lanes = pl.ds(pl.multiple_of(first * LANE, 2 * LANE), 2 * LANE)
        picked = nn(pick, drecv[:, lanes])
        strips = []
        for b in range(2):
            for c in range(4):
                strips.append(picked[c * 24 : c * 24 + 24, b * LANE : (b + 1) * LANE])
        strip = jnp.concatenate(strips, axis=1)
        features = pl.ds(pl.multiple_of(first * 512, 1024), 1024)
        rows_f[:, features] = strip
        left = strip[0:16].astype(BF16)
        h, a = nn(left, wiv[0, features, :]), nn(left, wot[features, :])
        hidden, act_grad = (h, a) if hidden is None else (hidden + h, act_grad + a)
    hidden, act_grad = hidden[0:8], act_grad[8:16]
    lhs = rows_f[0:16, :].astype(BF16)
    inner = slope_coef * (hidden + cubic_coef * hidden * hidden * hidden)
    tangent = jnp.tanh(inner)
    active = 0.5 * hidden * (1.0 + tangent)
    slope = 0.5 * (1.0 + tangent) + 0.5 * hidden * (1.0 - tangent * tangent) * slope_coef * (
        1.0 + 3.0 * cubic_coef * hidden * hidden
    )
    pre = act_grad * slope
    upper = iota((8, 256), 0) < 4
    none = jnp.zeros((8, 256), F32)
    active = jnp.where(upper, active, 0.0)
    pre = jnp.where(upper, 0.0, pre)
    active_lo = jnp.concatenate([active, none], axis=0).astype(BF16)
    active_hi = jnp.concatenate([none, active], axis=0).astype(BF16)
    pre_lo = jnp.concatenate([pre, none], axis=0).astype(BF16)
    result = (nn(active_lo, wov[0]) + nn(pre_lo, wit[...]))[0:8]
    wide = iota((8, 4096), 0) < 4
    dots = jnp.sum(result * (rows_f[0:8, :] + rows_f[16:24, :]), axis=1, keepdims=True)
    high = result.astype(BF16).astype(F32)
    rest = pltpu.roll(result - high, 4, 0)
    esend[...] = jnp.concatenate(
        [high, jnp.where(wide, rest, jnp.concatenate([spread(dots)] * 32, axis=1))], axis=0
    ).astype(BF16)

    def block(qq, e):
        return esend.at[:, pl.ds(pl.multiple_of((e * 4 + qq) * LANE, LANE), LANE)]

    scatter(block, erecv.at[r], 4)

    grad_w_out[0] = tn(active_hi, lhs).astype(BF16)
    grad_w_in[0] = tn(lhs, pre_lo).astype(BF16)

    arrived(erecv, 4)
    total = erecv[0].astype(F32)
    for k in range(1, NS):
        total = total + erecv[k].astype(F32)
    lower = iota((8, LANE), 0) < 4
    rest = pltpu.roll(total[8:16], 4, 0)
    dots = spread(jnp.sum(rest, axis=1, keepdims=True))
    fsend[...] = jnp.concatenate(
        [jnp.where(lower, total[0:8], total[0:8] + rest), jnp.where(lower, dots, 0.0)], axis=0
    ).astype(BF16)

    frows = pl.ds(pl.multiple_of(source * 16, 16), 16)
    flanes = pl.ds(pl.multiple_of(q * LANE, LANE), LANE)

    for d in ALONG_SEQ:
        remote(fsend, frecv.at[frows, flanes], 5, at_offset(*d), z).start()

    frecv[frows, flanes] = fsend[...]

    at = iota((96, LANE), 0)
    kind, slot = at // 32, lax.rem(at, 16)
    want = (slot // 2) * 16 + kind * 4 + (lax.rem(at, 32) // 16) * 2 + lax.rem(slot, 2)
    col = iota((96, LANE), 1)
    pick = jnp.where(col == want, 1.0, 0.0).astype(BF16)

    arrived(fwait, 5)
    picked = nn(pick, frecv[...])
    slot_out = picked[0:32].astype(BF16)
    input_grad = picked[32:64].astype(BF16)
    dots_b[...] = jnp.broadcast_to(jnp.sum(picked[64:96, 0:LANE], axis=1, keepdims=True), (32, LANE))
    for i in range(2):
        rows = slice(i * 16, i * 16 + 16)
        comb_part = nn(slot_out[rows], gvt[i])
        disp_part = nn(input_grad[rows], pvt[i])
        for b in range(4):
            lanes = slice(b * LANE, (b + 1) * LANE)
            gsend[i * 4 + b, 0:16] = comb_part[:, lanes].astype(BF16)
            gsend[i * 4 + b, 16:32] = disp_part[:, lanes].astype(BF16)

    for d in ALONG_EXP:
        zz = lax.rem(z + d, NZ)
        remote(gsend.at[zz], grecv.at[z], 6, r, zz).start()

    grecv[z] = gsend[z]
    chunk = logit[z]
    ec = jnp.exp(chunk - jnp.max(chunk, axis=0, keepdims=True))
    combine = ec / jnp.sum(ec, axis=0, keepdims=True)
    image = pl.ds(pl.multiple_of((z // 4) * 16, 16), 16)
    dispatch = jnp.exp(chunk - lse_b[image, :])
    col_dots = dots_b[image, :]
    arrived(grecv.at[pl.ds(0, NZ - 1)], 6)
    total = grecv[0].astype(F32)
    for k in range(1, NZ):
        total = total + grecv[k].astype(F32)
    comb_grad, disp_grad = total[0:16], total[16:32]
    row_dots = jnp.sum(combine * comb_grad, axis=0, keepdims=True)
    hbuf[z] = (combine * (comb_grad - row_dots) + dispatch * (disp_grad - col_dots)).astype(BF16)

    for d in ALONG_EXP:
        zz = lax.rem(z + d, NZ)
        remote(hbuf.at[z], hbuf.at[z], 7, r, zz).start()

    dispatch_b = []
    for i in range(2):
        li = jnp.concatenate([logit[i * 4 + b] for b in range(4)], axis=1)
        dispatch_b.append(jnp.exp(li - lse_col[i * 16 : i * 16 + 16]).astype(BF16))
    arrived(hbuf.at[pl.ds(0, NZ - 1)], 7)
    logit_b = [
        jnp.concatenate([hbuf[i * 4 + b] for b in range(4)], axis=1) for i in range(2)
    ]
    phi_part = nn(logit_b[0], pv[0]) + nn(logit_b[1], pv[1])
    for h in range(2):
        slots = slice(h * 8, h * 8 + 8)
        pair[h] = jnp.concatenate([phi_part[slots, 0:256], phi_part[slots, 256:512]], axis=0)

    def spread_patches(i):
        left = jnp.concatenate([dispatch_b[i], logit_b[i]], axis=0)
        right = jnp.concatenate([input_grad[i * 16 : i * 16 + 16], phi], axis=0)
        grad_patches[i] = tn(left, right).astype(BF16)

    trade = remote(pair.at[1 - core], paired, 8, sibling, z)
    trade.start()
    spread_patches(0)
    trade.wait_recv()
    half_sum = pair[core] + paired[...]
    isend[...] = half_sum.astype(BF16)
    for d in ALONG_SEQ:
        remote(isend, irecv.at[r], 9, at_offset(*d), z).start()
    irecv[r] = isend[...]
    spread_patches(1)
    arrived(irecv.at[pl.ds(0, NS - 1)], 9)
    for h in range(2):
        total = irecv[h].astype(F32)
        for k in range(1, 16):
            total = total + irecv[2 * k + h].astype(F32)
        total = total * (1.0 / math.sqrt(2 * 512 * NS))
        grad_phi[h * 8 : h * 8 + 8, 0:256] = total[0:8]
        grad_phi[h * 8 : h * 8 + 8, 256:512] = total[8:16]
    sent(asend.at[pl.ds(0, NZ - 1)], 0)
    sent(logit.at[pl.ds(0, NZ - 1)], 1)
    sent(dwait, 3)
    sent(fwait, 5)
    sent(gsend.at[pl.ds(0, NZ - 1)], 6)
    sent(hbuf.at[pl.ds(0, NZ - 1)], 7)
    trade.wait_send()
    sent(irecv.at[pl.ds(0, NS - 1)], 9)

    @pl.when(source == z)
    def _():
        sent(crecv.at[pl.ds(0, 16 * (NS - 1))], 2)
        sent(erecv.at[pl.ds(0, NS - 1)], 4)

    @pl.when(source != z)
    def _():
        sent(crecv, 2)
        sent(erecv, 4)


def store_kernel(gp, gphi, gwi, gwo, gp_out, gphi_out, gwi_out, gwo_out, sem):
    pieces = [(gphi, gphi_out)]
    for k in range(4):
        rows = pl.ds(k * 1024, 1024)
        pieces.append((gwi.at[:, rows], gwi_out.at[:, rows]))
        rows = pl.ds(k * 64, 64)
        pieces.append((gwo.at[:, rows], gwo_out.at[:, rows]))
    for k in range(2):
        pieces.append((gp.at[k], gp_out.at[k]))
    copies = [
        pltpu.make_async_copy(src, dst, sem.at[k]) for k, (src, dst) in enumerate(pieces)
    ]
    for copy in copies:
        copy.start()
    for copy in copies:
        copy.wait()


def local(patches, grad_out, phi_t, w_in, w_out):
    anywhere = pl.BlockSpec(memory_space=pl.ANY)
    hbm = pl.BlockSpec(memory_space=pltpu.HBM)

    def held(arrays, space):
        return [pltpu.with_memory_space_constraint(a, space) for a in arrays]

    vmem = pltpu.VMEM
    shapes = (
        jax.ShapeDtypeStruct(patches.shape, BF16),
        jax.ShapeDtypeStruct(phi_t.shape, F32),
        jax.ShapeDtypeStruct(w_in.shape, BF16),
        jax.ShapeDtypeStruct(w_out.shape, BF16),
    )
    results = pl.pallas_call(
        kernel,
        out_shape=shapes,
        in_specs=[hbm] * 5,
        out_specs=[pl.BlockSpec(memory_space=pltpu.VMEM)] * 4,
        scratch_shapes=[
            vmem((2, 512, 512), BF16),
            vmem((2, 512, 512), BF16),
            vmem((16, 512), BF16),
            vmem((1, 4096, 256), BF16),
            vmem((1, 256, 4096), BF16),
            vmem((2, 512, 512), BF16),
            vmem((2, 512, 512), BF16),
            vmem((256, 4096), BF16),
            vmem((4096, 256), BF16),
            vmem((8, 16, LANE), F32),
            vmem((8, 16, LANE), F32),
            vmem((8, 16, LANE), F32),
            vmem((512, LANE), F32),
            vmem((512, LANE), BF16),
            vmem((512, LANE), BF16),
            vmem((16, LANE), F32),
            vmem((16, LANE), BF16),
            vmem((64, 1024), BF16),
            vmem((24, 4096), F32),
            vmem((16, 4096), BF16),
            vmem((32, 16, LANE), BF16),
            vmem((16, LANE), BF16),
            vmem((LANE, 512), BF16),
            vmem((32, LANE), F32),
            vmem((32, LANE), F32),
            vmem((8, 32, LANE), BF16),
            vmem((8, 32, LANE), BF16),
            vmem((8, 16, LANE), BF16),
            vmem((2, 16, 256), F32),
            vmem((16, 256), F32),
            vmem((16, 256), BF16),
            vmem((32, 16, 256), BF16),
            pltpu.SemaphoreType.DMA((6,)),
            pltpu.SemaphoreType.DMA((10,)),
            pltpu.SemaphoreType.DMA((10,)),
            pltpu.SemaphoreType.DMA((4,)),
            pltpu.SemaphoreType.REGULAR((3,)),
        ],
        compiler_params=pltpu.CompilerParams(
            collective_id=0, has_side_effects=True, vmem_limit_bytes=28 * 1024 * 1024
        ),
        cost_estimate=pl.CostEstimate(
            flops=400_000_000, bytes_accessed=12_000_000, transcendentals=100_000
        ),
    )(*held((patches, grad_out, phi_t, w_in, w_out), pltpu.HBM))
    return pl.pallas_call(
        store_kernel,
        out_shape=shapes,
        in_specs=[anywhere] * 4,
        out_specs=[hbm] * 4,
        scratch_shapes=[pltpu.SemaphoreType.DMA((11,))],
        compiler_params=pltpu.CompilerParams(vmem_limit_bytes=4 * 1024 * 1024),
    )(*held(results, pltpu.VMEM))


def solution(mesh):
    in_specs = (
        P(None, "seq", "exp"),
        P(None, "seq", "exp"),
        P(None, "exp"),
        P("exp", None, "seq"),
        P("exp", "seq", None),
    )
    out_specs = (
        P(None, "seq", "exp"),
        P(None, "exp"),
        P("exp", None, "seq"),
        P("exp", "seq", None),
    )
    return jax.shard_map(local, mesh=mesh, in_specs=in_specs, out_specs=out_specs, check_vma=False)
```

```python
import math

import jax
import jax.numpy as jnp
from jax import lax
from jax.experimental import pallas as pl
from jax.experimental.pallas import tpu as pltpu
from jax.sharding import PartitionSpec as P

MESH = pl.DeviceIdType.MESH
F32 = jnp.float32
BF16 = jnp.bfloat16

slope_coef = 0.7978845608
cubic_coef = 0.044715

NS = 32
NZ = 8
LANE = 128


def ring(d, n):
    return min(d, n - d)


ALONG_EXP = sorted(range(1, NZ), key=lambda d: -ring(d, NZ))
CHIPS = sorted(
    ((dy, dx) for dy in range(4) for dx in range(4)), key=lambda d: -ring(d[0], 4) - ring(d[1], 4)
)
ALONG_SEQ = [(dy, dx, dc) for dy, dx in CHIPS for dc in range(2) if (dy, dx, dc) != (0, 0, 0)]


def nn(a, b):
    return lax.dot_general(a, b, (((1,), (0,)), ((), ())), preferred_element_type=F32)


def nt(a, b):
    return lax.dot_general(a, b, (((1,), (1,)), ((), ())), preferred_element_type=F32)


def tn(a, b):
    return lax.dot_general(a, b, (((0,), (0,)), ((), ())), preferred_element_type=F32)


def iota(shape, dim):
    return lax.broadcasted_iota(jnp.int32, shape, dim)


def thirds(value):
    first = value.astype(BF16).astype(F32)
    second = (value - first).astype(BF16).astype(F32)
    return first, second, value - first - second


def spread(column):
    first, second, third = thirds(column)
    lane = iota((8, LANE), 1)
    return jnp.where(
        lane == 0, first, jnp.where(lane == 1, second, jnp.where(lane == 2, third, 0.0))
    )


def kernel(
    patches, grad_out, phi_t, w_in, w_out,
    grad_patches, grad_phi, grad_w_in, grad_w_out,
    pv, gv, phv, wiv, wov, pvt, gvt, wit, wot,
    asend, arecv, logit, cfull, csend, crecv, dtmp, dsend, drecv, rows_f,
    esend, erecv, fsend, frecv, lse_b, dots_b, gsend, grecv, hbuf, pair, paired, isend, irecv, halves,
    in_sem, send_sem, recv_sem, d_sem, known,
):
    r = lax.axis_index("seq")
    z = lax.axis_index("exp")
    source, q = r // 4, lax.rem(r, 4)

    y, x, core = r // 8, lax.rem(r // 2, 4), lax.rem(r, 2)

    def at_offset(dy, dx, dc):
        return (lax.rem(y + dy, 4) * 4 + lax.rem(x + dx, 4)) * 2 + lax.rem(core + dc, 2)

    loads = [
        pltpu.make_async_copy(src, dst, in_sem.at[k])
        for k, (src, dst) in enumerate(
            [
                (phi_t, phv), (patches.at[0], pv.at[0]), (patches.at[1], pv.at[1]),
                (grad_out, gv), (w_out, wov), (w_in, wiv),
            ]
        )
    ]
    for load in loads[:3]:
        load.start()

    barrier = pltpu.get_barrier_semaphore()

    def greet(rr, zz):
        pl.semaphore_signal(barrier, inc=1, device_id=(rr, zz), device_id_type=MESH)

    x_line = [at_offset(0, d, 0) for d in (2, 1, 3)]
    y_line = [at_offset(d, 0, 0) for d in (2, 1, 3)]
    sibling = at_offset(0, 0, 1)

    for d in ALONG_EXP:
        greet(r, lax.rem(z + d, NZ))
    for rr in x_line + y_line + [sibling]:
        greet(rr, z)

    def tell(line, step):
        for rr in line:
            pl.semaphore_signal(known.at[step], inc=1, device_id=(rr, z), device_id_type=MESH)

    def remote(src, dst, phase, rr, zz):
        return pltpu.make_async_remote_copy(
            src_ref=src,
            dst_ref=dst,
            send_sem=send_sem.at[phase],
            recv_sem=recv_sem.at[phase],
            device_id=(rr, zz),
            device_id_type=MESH,
        )

    def arrived(ref, phase):
        pltpu.make_async_copy(ref, ref, recv_sem.at[phase]).wait()

    dwait = fwait = csend.at[pl.ds(0, 16 * (NS - 1))]

    def sent(ref, phase):
        pltpu.make_async_copy(ref, ref, send_sem.at[phase]).wait()

    def scatter(piece, place, phase):
        for d in ALONG_EXP:
            e = lax.rem(z + d, NZ)
            for k in range(4):
                qq = lax.rem(r + k, 4)
                remote(piece(qq, e), place, phase, z * 4 + qq, e).start()
        for k in range(4):
            qq = lax.rem(r + k, 4)
            rr = z * 4 + qq

            @pl.when(rr != r)
            def _():
                remote(piece(qq, z), place, phase, rr, z).start()

            @pl.when(rr == r)
            def _():
                pltpu.make_async_copy(piece(qq, z), place, recv_sem.at[phase]).start()

    loads[0].wait()
    phi = phv[...]
    for i in range(2):
        loads[1 + i].wait()
        part = nt(phi, pv[i])
        for b in range(4):
            asend[i * 4 + b] = part[:, b * LANE : (b + 1) * LANE]
    for load in loads[3:]:
        load.start()

    pl.semaphore_wait(barrier, NZ - 1 + 7)

    for d in ALONG_EXP:
        zz = lax.rem(z + d, NZ)
        remote(asend.at[zz], arecv.at[z], 0, r, zz).start()

    arecv[z] = asend[z]
    tell([sibling], 0)
    pl.semaphore_wait(known.at[0], 1)
    tell(x_line, 1)
    loads[4].wait()
    wot[...] = wov[0].T
    arrived(arecv.at[pl.ds(0, NZ - 1)], 0)
    total = arecv[0]
    for k in range(1, NZ):
        total = total + arecv[k]
    logit[z] = total

    for d in ALONG_EXP:
        zz = lax.rem(z + d, NZ)
        remote(logit.at[z], logit.at[z], 1, r, zz).start()

    pl.semaphore_wait(known.at[1], 3)
    tell(y_line, 2)
    loads[5].wait()
    wit[...] = wiv[0].T
    loads[3].wait()
    arrived(logit.at[pl.ds(0, NZ - 1)], 1)
    pl.semaphore_wait(known.at[2], 3)

    diag = iota((32, LANE), 0) == iota((32, LANE), 1)
    peaks, sums = [], []
    for i in range(2):
        li = jnp.concatenate([logit[i * 4 + b] for b in range(4)], axis=1)
        peak = jnp.max(li, axis=1, keepdims=True).astype(BF16).astype(F32)
        e = jnp.exp(li - peak)
        peaks.append(peak)
        sums.append(jnp.sum(e, axis=1, keepdims=True))
        hi = e.astype(BF16)
        lo = (e - hi.astype(F32)).astype(BF16)
        both = nn(jnp.concatenate([hi, lo], axis=0), pv[i])
        slot_part = both[:16] + both[16:]
        ec = jnp.exp(li - jnp.max(li, axis=0, keepdims=True))
        combine_b = (ec / jnp.sum(ec, axis=0, keepdims=True)).astype(BF16)
        grad_part = nn(combine_b, gv[i])
        for half in range(2):
            for c in range(4):
                base = (i * 16 + half * 8) * 16 + c
                rows = slice(half * 8, half * 8 + 8)
                lanes = slice(c * LANE, (c + 1) * LANE)
                high = slot_part[rows, lanes].astype(BF16).astype(F32)
                cfull[pl.ds(base, 8, stride=16), :] = high
                cfull[pl.ds(base + 4, 8, stride=16), :] = slot_part[rows, lanes] - high
                cfull[pl.ds(base + 8, 8, stride=16), :] = grad_part[rows, lanes]
    peak_col = jnp.concatenate(peaks, axis=0)
    sum_col = jnp.concatenate(sums, axis=0)
    peak_row = jnp.sum(jnp.where(diag, peak_col, 0.0), axis=0, keepdims=True)
    sum_row = jnp.sum(jnp.where(diag, sum_col, 0.0), axis=0, keepdims=True)
    stats = (peak_row,) + thirds(sum_row)
    for k, row in enumerate(stats):
        cfull[pl.ds(12 + k, 32, stride=16), :] = jnp.broadcast_to(row, (32, LANE))
    csend[...] = cfull[...].astype(BF16)

    def piece(qq, e):
        row = (qq // 2) * 16 + e * 2 + lax.rem(qq, 2)
        return csend.at[pl.ds(pl.multiple_of(row * 16, 16), 16)]

    scatter(piece, crecv.at[pl.ds(pl.multiple_of(r * 16, 16), 16)], 2)
    for i in range(2):
        pvt[i] = pv[i].T
        gvt[i] = gv[i].T
    arrived(crecv, 2)
    cfull[...] = crecv[...].astype(F32)
    peak_all = cfull[pl.ds(12, 32, stride=16), :]
    sum_all = (
        cfull[pl.ds(13, 32, stride=16), :]
        + cfull[pl.ds(14, 32, stride=16), :]
        + cfull[pl.ds(15, 32, stride=16), :]
    )
    top = jnp.max(peak_all, axis=0, keepdims=True)
    scale = jnp.exp(peak_all - top)
    denom = jnp.sum(scale * sum_all, axis=0, keepdims=True)
    lse_row = top + jnp.log(denom)
    lse_col = jnp.sum(jnp.where(diag, lse_row, 0.0), axis=1, keepdims=True)
    lse_b[...] = jnp.broadcast_to(lse_col, (32, LANE))
    mine = (q // 2) * 16 + z * 2 + lax.rem(q, 2)
    weight = jnp.sum(
        jnp.where(iota((32, LANE), 1) == mine, scale / denom, 0.0), axis=1, keepdims=True
    )
    dtmp[...] = jnp.zeros((16, LANE), F32)
    for c in range(4):
        part = cfull[pl.ds(c, 32, stride=16), :] + cfull[pl.ds(4 + c, 32, stride=16), :]
        row = jnp.sum(weight * part, axis=0, keepdims=True)
        high = row.astype(BF16).astype(F32)
        dtmp[c : c + 1, :] = high
        dtmp[4 + c : 5 + c, :] = row - high
        dtmp[8 + c : 9 + c, :] = jnp.sum(
            cfull[pl.ds(8 + c, 32, stride=16), :], axis=0, keepdims=True
        )
    dsend[...] = dtmp[...].astype(BF16)

    drows = pl.ds(pl.multiple_of(q * 16, 16), 16)
    dlanes = pl.ds(pl.multiple_of(source * LANE, LANE), LANE)

    for dy, dx, dc in ALONG_SEQ[::-1]:
        pltpu.make_async_remote_copy(
            src_ref=dsend,
            dst_ref=drecv.at[drows, dlanes],
            send_sem=send_sem.at[3],
            recv_sem=d_sem.at[(4 - dy) % 4],
            device_id=(at_offset(dy, dx, dc), z),
            device_id_type=MESH,
        ).start()

    drecv[drows, dlanes] = dsend[...]

    at = iota((96, 64), 0)
    c_of, j = at // 24, lax.rem(at, 24)
    part_of = jnp.where(j < 8, 0, jnp.where(j < 16, 8, 4))
    want = lax.rem(j, 4) * 16 + part_of + c_of
    pick = jnp.where(iota((96, 64), 1) == want, 1.0, 0.0).astype(BF16)

    hidden = act_grad = None
    for g in (0, 1, 3, 2):
        come = csend.at[pl.ds(0, 16 * (7 if g == 0 else 8))]
        pltpu.make_async_copy(come, come, d_sem.at[g]).wait()
        first = lax.rem(y + g, 4) * 2
        lanes = pl.ds(pl.multiple_of(first * LANE, 2 * LANE), 2 * LANE)
        picked = nn(pick, drecv[:, lanes])
        strips = []
        for b in range(2):
            for c in range(4):
                strips.append(picked[c * 24 : c * 24 + 24, b * LANE : (b + 1) * LANE])
        strip = jnp.concatenate(strips, axis=1)
        features = pl.ds(pl.multiple_of(first * 512, 1024), 1024)
        rows_f[:, features] = strip
        left = strip[0:16].astype(BF16)
        h, a = nn(left, wiv[0, features, :]), nn(left, wot[features, :])
        hidden, act_grad = (h, a) if hidden is None else (hidden + h, act_grad + a)
    hidden, act_grad = hidden[0:8], act_grad[8:16]
    lhs = rows_f[0:16, :].astype(BF16)
    inner = slope_coef * (hidden + cubic_coef * hidden * hidden * hidden)
    tangent = jnp.tanh(inner)
    active = 0.5 * hidden * (1.0 + tangent)
    slope = 0.5 * (1.0 + tangent) + 0.5 * hidden * (1.0 - tangent * tangent) * slope_coef * (
        1.0 + 3.0 * cubic_coef * hidden * hidden
    )
    pre = act_grad * slope
    upper = iota((8, 256), 0) < 4
    none = jnp.zeros((8, 256), F32)
    active = jnp.where(upper, active, 0.0)
    pre = jnp.where(upper, 0.0, pre)
    active_lo = jnp.concatenate([active, none], axis=0).astype(BF16)
    active_hi = jnp.concatenate([none, active], axis=0).astype(BF16)
    pre_lo = jnp.concatenate([pre, none], axis=0).astype(BF16)
    result = (nn(active_lo, wov[0]) + nn(pre_lo, wit[...]))[0:8]
    wide = iota((8, 4096), 0) < 4
    dots = jnp.sum(result * (rows_f[0:8, :] + rows_f[16:24, :]), axis=1, keepdims=True)
    high = result.astype(BF16).astype(F32)
    rest = pltpu.roll(result - high, 4, 0)
    esend[...] = jnp.concatenate(
        [high, jnp.where(wide, rest, jnp.concatenate([spread(dots)] * 32, axis=1))], axis=0
    ).astype(BF16)

    def block(qq, e):
        return esend.at[:, pl.ds(pl.multiple_of((e * 4 + qq) * LANE, LANE), LANE)]

    scatter(block, erecv.at[r], 4)

    grad_w_out[0] = tn(active_hi, lhs).astype(BF16)
    grad_w_in[0] = tn(lhs, pre_lo).astype(BF16)

    arrived(erecv, 4)
    total = erecv[0].astype(F32)
    for k in range(1, NS):
        total = total + erecv[k].astype(F32)
    lower = iota((8, LANE), 0) < 4
    rest = pltpu.roll(total[8:16], 4, 0)
    dots = spread(jnp.sum(rest, axis=1, keepdims=True))
    fsend[...] = jnp.concatenate(
        [jnp.where(lower, total[0:8], total[0:8] + rest), jnp.where(lower, dots, 0.0)], axis=0
    ).astype(BF16)

    frows = pl.ds(pl.multiple_of(source * 16, 16), 16)
    flanes = pl.ds(pl.multiple_of(q * LANE, LANE), LANE)

    for d in ALONG_SEQ[::-1]:
        remote(fsend, frecv.at[frows, flanes], 5, at_offset(*d), z).start()

    frecv[frows, flanes] = fsend[...]

    at = iota((96, LANE), 0)
    kind, slot = at // 32, lax.rem(at, 16)
    want = (slot // 2) * 16 + kind * 4 + (lax.rem(at, 32) // 16) * 2 + lax.rem(slot, 2)
    col = iota((96, LANE), 1)
    pick = jnp.where(col == want, 1.0, 0.0).astype(BF16)

    arrived(fwait, 5)
    picked = nn(pick, frecv[...])
    slot_out = picked[0:32].astype(BF16)
    input_grad = picked[32:64].astype(BF16)
    dots_b[...] = jnp.broadcast_to(jnp.sum(picked[64:96, 0:LANE], axis=1, keepdims=True), (32, LANE))
    for i in range(2):
        rows = slice(i * 16, i * 16 + 16)
        comb_part = nn(slot_out[rows], gvt[i])
        disp_part = nn(input_grad[rows], pvt[i])
        for b in range(4):
            lanes = slice(b * LANE, (b + 1) * LANE)
            gsend[i * 4 + b, 0:16] = comb_part[:, lanes].astype(BF16)
            gsend[i * 4 + b, 16:32] = disp_part[:, lanes].astype(BF16)

    for d in ALONG_EXP:
        zz = lax.rem(z + d, NZ)
        remote(gsend.at[zz], grecv.at[z], 6, r, zz).start()

    grecv[z] = gsend[z]
    chunk = logit[z]
    ec = jnp.exp(chunk - jnp.max(chunk, axis=0, keepdims=True))
    combine = ec / jnp.sum(ec, axis=0, keepdims=True)
    image = pl.ds(pl.multiple_of((z // 4) * 16, 16), 16)
    dispatch = jnp.exp(chunk - lse_b[image, :])
    col_dots = dots_b[image, :]
    arrived(grecv.at[pl.ds(0, NZ - 1)], 6)
    total = grecv[0].astype(F32)
    for k in range(1, NZ):
        total = total + grecv[k].astype(F32)
    comb_grad, disp_grad = total[0:16], total[16:32]
    row_dots = jnp.sum(combine * comb_grad, axis=0, keepdims=True)
    hbuf[z] = (combine * (comb_grad - row_dots) + dispatch * (disp_grad - col_dots)).astype(BF16)

    for d in ALONG_EXP:
        zz = lax.rem(z + d, NZ)
        remote(hbuf.at[z], hbuf.at[z], 7, r, zz).start()

    dispatch_b = []
    for i in range(2):
        li = jnp.concatenate([logit[i * 4 + b] for b in range(4)], axis=1)
        dispatch_b.append(jnp.exp(li - lse_col[i * 16 : i * 16 + 16]).astype(BF16))
    arrived(hbuf.at[pl.ds(0, NZ - 1)], 7)
    logit_b = [
        jnp.concatenate([hbuf[i * 4 + b] for b in range(4)], axis=1) for i in range(2)
    ]
    phi_part = nn(logit_b[0], pv[0]) + nn(logit_b[1], pv[1])
    for h in range(2):
        slots = slice(h * 8, h * 8 + 8)
        pair[h] = jnp.concatenate([phi_part[slots, 0:256], phi_part[slots, 256:512]], axis=0)

    def spread_patches(i):
        left = jnp.concatenate([dispatch_b[i], logit_b[i]], axis=0)
        right = jnp.concatenate([input_grad[i * 16 : i * 16 + 16], phi], axis=0)
        grad_patches[i] = tn(left, right).astype(BF16)

    trade = remote(pair.at[1 - core], paired, 8, sibling, z)
    trade.start()
    spread_patches(0)
    trade.wait_recv()
    half_sum = pair[core] + paired[...]
    isend[...] = half_sum.astype(BF16)
    for dy, dx in CHIPS[:-1]:
        remote(isend, irecv.at[r // 2], 9, at_offset(dy, dx, 0), z).start()
    irecv[r // 2] = isend[...]
    spread_patches(1)
    arrived(irecv.at[pl.ds(0, 15)], 9)
    total = irecv[0].astype(F32)
    for k in range(1, 16):
        total = total + irecv[k].astype(F32)
    halves[core] = total * (1.0 / math.sqrt(2 * 512 * NS))
    back = remote(halves.at[core], halves.at[core], 10, sibling, z)
    back.start()
    sent(asend.at[pl.ds(0, NZ - 1)], 0)
    sent(logit.at[pl.ds(0, NZ - 1)], 1)
    sent(dwait, 3)
    sent(fwait, 5)
    sent(gsend.at[pl.ds(0, NZ - 1)], 6)
    sent(hbuf.at[pl.ds(0, NZ - 1)], 7)
    trade.wait_send()
    sent(irecv.at[pl.ds(0, 15)], 9)

    @pl.when(source == z)
    def _():
        sent(crecv.at[pl.ds(0, 16 * (NS - 1))], 2)
        sent(erecv.at[pl.ds(0, NS - 1)], 4)

    @pl.when(source != z)
    def _():
        sent(crecv, 2)
        sent(erecv, 4)

    back.wait()
    for h in range(2):
        grad_phi[h * 8 : h * 8 + 8, 0:256] = halves[h, 0:8]
        grad_phi[h * 8 : h * 8 + 8, 256:512] = halves[h, 8:16]


def store_kernel(gp, gphi, gwi, gwo, gp_out, gphi_out, gwi_out, gwo_out, sem):
    pieces = [(gphi, gphi_out)]
    for k in range(4):
        rows = pl.ds(k * 1024, 1024)
        pieces.append((gwi.at[:, rows], gwi_out.at[:, rows]))
        rows = pl.ds(k * 64, 64)
        pieces.append((gwo.at[:, rows], gwo_out.at[:, rows]))
    for k in range(2):
        pieces.append((gp.at[k], gp_out.at[k]))
    copies = [
        pltpu.make_async_copy(src, dst, sem.at[k]) for k, (src, dst) in enumerate(pieces)
    ]
    for copy in copies:
        copy.start()
    for copy in copies:
        copy.wait()


def local(patches, grad_out, phi_t, w_in, w_out):
    anywhere = pl.BlockSpec(memory_space=pl.ANY)
    hbm = pl.BlockSpec(memory_space=pltpu.HBM)

    def held(arrays, space):
        return [pltpu.with_memory_space_constraint(a, space) for a in arrays]

    vmem = pltpu.VMEM
    shapes = (
        jax.ShapeDtypeStruct(patches.shape, BF16),
        jax.ShapeDtypeStruct(phi_t.shape, F32),
        jax.ShapeDtypeStruct(w_in.shape, BF16),
        jax.ShapeDtypeStruct(w_out.shape, BF16),
    )
    results = pl.pallas_call(
        kernel,
        out_shape=shapes,
        in_specs=[hbm] * 5,
        out_specs=[pl.BlockSpec(memory_space=pltpu.VMEM)] * 4,
        scratch_shapes=[
            vmem((2, 512, 512), BF16),
            vmem((2, 512, 512), BF16),
            vmem((16, 512), BF16),
            vmem((1, 4096, 256), BF16),
            vmem((1, 256, 4096), BF16),
            vmem((2, 512, 512), BF16),
            vmem((2, 512, 512), BF16),
            vmem((256, 4096), BF16),
            vmem((4096, 256), BF16),
            vmem((8, 16, LANE), F32),
            vmem((8, 16, LANE), F32),
            vmem((8, 16, LANE), F32),
            vmem((512, LANE), F32),
            vmem((512, LANE), BF16),
            vmem((512, LANE), BF16),
            vmem((16, LANE), F32),
            vmem((16, LANE), BF16),
            vmem((64, 1024), BF16),
            vmem((24, 4096), F32),
            vmem((16, 4096), BF16),
            vmem((32, 16, LANE), BF16),
            vmem((16, LANE), BF16),
            vmem((LANE, 512), BF16),
            vmem((32, LANE), F32),
            vmem((32, LANE), F32),
            vmem((8, 32, LANE), BF16),
            vmem((8, 32, LANE), BF16),
            vmem((8, 16, LANE), BF16),
            vmem((2, 16, 256), F32),
            vmem((16, 256), F32),
            vmem((16, 256), BF16),
            vmem((16, 16, 256), BF16),
            vmem((2, 16, 256), F32),
            pltpu.SemaphoreType.DMA((6,)),
            pltpu.SemaphoreType.DMA((11,)),
            pltpu.SemaphoreType.DMA((11,)),
            pltpu.SemaphoreType.DMA((4,)),
            pltpu.SemaphoreType.REGULAR((3,)),
        ],
        compiler_params=pltpu.CompilerParams(
            collective_id=0, has_side_effects=True, vmem_limit_bytes=28 * 1024 * 1024
        ),
        cost_estimate=pl.CostEstimate(
            flops=400_000_000, bytes_accessed=12_000_000, transcendentals=100_000
        ),
    )(*held((patches, grad_out, phi_t, w_in, w_out), pltpu.HBM))
    return pl.pallas_call(
        store_kernel,
        out_shape=shapes,
        in_specs=[anywhere] * 4,
        out_specs=[hbm] * 4,
        scratch_shapes=[pltpu.SemaphoreType.DMA((11,))],
        compiler_params=pltpu.CompilerParams(vmem_limit_bytes=4 * 1024 * 1024),
    )(*held(results, pltpu.VMEM))


def solution(mesh):
    in_specs = (
        P(None, "seq", "exp"),
        P(None, "seq", "exp"),
        P(None, "exp"),
        P("exp", None, "seq"),
        P("exp", "seq", None),
    )
    out_specs = (
        P(None, "seq", "exp"),
        P(None, "exp"),
        P("exp", None, "seq"),
        P("exp", "seq", None),
    )
    return jax.shard_map(local, mesh=mesh, in_specs=in_specs, out_specs=out_specs, check_vma=False)
```

```python
import math

import jax
import jax.numpy as jnp
from jax import lax
from jax.experimental import pallas as pl
from jax.experimental.pallas import tpu as pltpu
from jax.sharding import PartitionSpec as P

MESH = pl.DeviceIdType.MESH
F32 = jnp.float32
BF16 = jnp.bfloat16

slope_coef = 0.7978845608
cubic_coef = 0.044715

NS = 32
NZ = 8
LANE = 128


def ring(d, n):
    return min(d, n - d)


ALONG_EXP = sorted(range(1, NZ), key=lambda d: -ring(d, NZ))
CHIPS = sorted(
    ((dy, dx) for dy in range(4) for dx in range(4)), key=lambda d: -ring(d[0], 4) - ring(d[1], 4)
)
ALONG_SEQ = [(dy, dx, dc) for dy, dx in CHIPS for dc in range(2) if (dy, dx, dc) != (0, 0, 0)]


def nn(a, b):
    return lax.dot_general(a, b, (((1,), (0,)), ((), ())), preferred_element_type=F32)


def nt(a, b):
    return lax.dot_general(a, b, (((1,), (1,)), ((), ())), preferred_element_type=F32)


def tn(a, b):
    return lax.dot_general(a, b, (((0,), (0,)), ((), ())), preferred_element_type=F32)


def iota(shape, dim):
    return lax.broadcasted_iota(jnp.int32, shape, dim)


def thirds(value):
    first = value.astype(BF16).astype(F32)
    second = (value - first).astype(BF16).astype(F32)
    return first, second, value - first - second


def kernel(
    patches, grad_out, phi_t, w_in, w_out,
    grad_patches, grad_phi, grad_w_in, grad_w_out,
    pv, gv, phv, wiv, wov, pvt, gvt, wit, wot,
    asend, arecv, logit, cfull, csend, crecv, dtmp, dsend, drecv, rows_f,
    esend, erecv, fsend, frecv, lse_b, dots_b, gsend, grecv, hbuf, pair, paired, isend, irecv, halves,
    in_sem, send_sem, recv_sem, d_sem, known,
):
    r = lax.axis_index("seq")
    z = lax.axis_index("exp")
    source, q = r // 4, lax.rem(r, 4)

    y, x, core = r // 8, lax.rem(r // 2, 4), lax.rem(r, 2)

    def at_offset(dy, dx, dc):
        return (lax.rem(y + dy, 4) * 4 + lax.rem(x + dx, 4)) * 2 + lax.rem(core + dc, 2)

    def along(d):
        return lax.rem(z + jnp.where(core == 0, d, NZ - d), NZ)

    loads = [
        pltpu.make_async_copy(src, dst, in_sem.at[k])
        for k, (src, dst) in enumerate(
            [
                (phi_t, phv), (patches.at[0], pv.at[0]), (patches.at[1], pv.at[1]),
                (grad_out, gv), (w_out, wov), (w_in, wiv),
            ]
        )
    ]
    for load in loads[:3]:
        load.start()

    barrier = pltpu.get_barrier_semaphore()

    def greet(rr, zz):
        pl.semaphore_signal(barrier, inc=1, device_id=(rr, zz), device_id_type=MESH)

    x_line = [at_offset(0, d, 0) for d in (2, 1, 3)]
    y_line = [at_offset(d, 0, 0) for d in (2, 1, 3)]
    sibling = at_offset(0, 0, 1)

    for d in ALONG_EXP:
        greet(r, lax.rem(z + d, NZ))
    for rr in x_line + y_line + [sibling]:
        greet(rr, z)

    def tell(line, step):
        for rr in line:
            pl.semaphore_signal(known.at[step], inc=1, device_id=(rr, z), device_id_type=MESH)

    def remote(src, dst, phase, rr, zz):
        return pltpu.make_async_remote_copy(
            src_ref=src,
            dst_ref=dst,
            send_sem=send_sem.at[phase],
            recv_sem=recv_sem.at[phase],
            device_id=(rr, zz),
            device_id_type=MESH,
        )

    def arrived(ref, phase):
        pltpu.make_async_copy(ref, ref, recv_sem.at[phase]).wait()

    dwait = fwait = csend.at[pl.ds(0, 16 * (NS - 1))]

    def sent(ref, phase):
        pltpu.make_async_copy(ref, ref, send_sem.at[phase]).wait()

    def scatter(piece, place, phase):
        for d in ALONG_EXP:
            e = lax.rem(z + d, NZ)
            for k in range(4):
                qq = lax.rem(r + k, 4)
                remote(piece(qq, e), place, phase, z * 4 + qq, e).start()
        for k in range(4):
            qq = lax.rem(r + k, 4)
            rr = z * 4 + qq

            @pl.when(rr != r)
            def _():
                remote(piece(qq, z), place, phase, rr, z).start()

            @pl.when(rr == r)
            def _():
                pltpu.make_async_copy(piece(qq, z), place, recv_sem.at[phase]).start()

    loads[0].wait()
    phi = phv[...]
    for i in range(2):
        loads[1 + i].wait()
        part = nt(phi, pv[i])
        for b in range(4):
            asend[i * 4 + b] = part[:, b * LANE : (b + 1) * LANE]
    for load in loads[3:]:
        load.start()

    pl.semaphore_wait(barrier, NZ - 1 + 7)

    for d in ALONG_EXP:
        zz = along(d)
        remote(asend.at[zz], arecv.at[z], 0, r, zz).start()

    arecv[z] = asend[z]
    tell([sibling], 0)
    pl.semaphore_wait(known.at[0], 1)
    tell(x_line, 1)
    arrived(arecv.at[pl.ds(0, NZ - 1)], 0)
    total = arecv[0]
    for k in range(1, NZ):
        total = total + arecv[k]
    logit[z] = total

    for d in ALONG_EXP:
        zz = along(d)
        remote(logit.at[z], logit.at[z], 1, r, zz).start()

    pl.semaphore_wait(known.at[1], 3)
    tell(y_line, 2)
    loads[3].wait()
    arrived(logit.at[pl.ds(0, NZ - 1)], 1)
    pl.semaphore_wait(known.at[2], 3)

    diag = iota((32, LANE), 0) == iota((32, LANE), 1)
    peaks, sums = [], []
    for i in range(2):
        li = jnp.concatenate([logit[i * 4 + b] for b in range(4)], axis=1)
        peak = jnp.max(li, axis=1, keepdims=True).astype(BF16).astype(F32)
        e = jnp.exp(li - peak)
        peaks.append(peak)
        sums.append(jnp.sum(e, axis=1, keepdims=True))
        hi = e.astype(BF16)
        lo = (e - hi.astype(F32)).astype(BF16)
        both = nn(jnp.concatenate([hi, lo], axis=0), pv[i])
        slot_part = both[:16] + both[16:]
        ec = jnp.exp(li - jnp.max(li, axis=0, keepdims=True))
        combine_b = (ec / jnp.sum(ec, axis=0, keepdims=True)).astype(BF16)
        grad_part = nn(combine_b, gv[i])
        for half in range(2):
            for c in range(4):
                base = (i * 16 + half * 8) * 16 + c
                rows = slice(half * 8, half * 8 + 8)
                lanes = slice(c * LANE, (c + 1) * LANE)
                high = slot_part[rows, lanes].astype(BF16).astype(F32)
                cfull[pl.ds(base, 8, stride=16), :] = high
                cfull[pl.ds(base + 4, 8, stride=16), :] = slot_part[rows, lanes] - high
                cfull[pl.ds(base + 8, 8, stride=16), :] = grad_part[rows, lanes]
    peak_col = jnp.concatenate(peaks, axis=0)
    sum_col = jnp.concatenate(sums, axis=0)
    peak_row = jnp.sum(jnp.where(diag, peak_col, 0.0), axis=0, keepdims=True)
    sum_row = jnp.sum(jnp.where(diag, sum_col, 0.0), axis=0, keepdims=True)
    stats = (peak_row,) + thirds(sum_row)
    for k, row in enumerate(stats):
        cfull[pl.ds(12 + k, 32, stride=16), :] = jnp.broadcast_to(row, (32, LANE))
    csend[...] = cfull[...].astype(BF16)

    def piece(qq, e):
        row = (qq // 2) * 16 + e * 2 + lax.rem(qq, 2)
        return csend.at[pl.ds(pl.multiple_of(row * 16, 16), 16)]

    scatter(piece, crecv.at[pl.ds(pl.multiple_of(r * 16, 16), 16)], 2)
    loads[4].wait()
    wot[...] = wov[0].T
    loads[5].wait()
    wit[...] = wiv[0].T
    arrived(crecv, 2)
    cfull[...] = crecv[...].astype(F32)
    peak_all = cfull[pl.ds(12, 32, stride=16), :]
    sum_all = (
        cfull[pl.ds(13, 32, stride=16), :]
        + cfull[pl.ds(14, 32, stride=16), :]
        + cfull[pl.ds(15, 32, stride=16), :]
    )
    top = jnp.max(peak_all, axis=0, keepdims=True)
    scale = jnp.exp(peak_all - top)
    denom = jnp.sum(scale * sum_all, axis=0, keepdims=True)
    lse_row = top + jnp.log(denom)
    lse_col = jnp.sum(jnp.where(diag, lse_row, 0.0), axis=1, keepdims=True)
    lse_b[...] = jnp.broadcast_to(lse_col, (32, LANE))
    mine = (q // 2) * 16 + z * 2 + lax.rem(q, 2)
    weight = jnp.sum(
        jnp.where(iota((32, LANE), 1) == mine, scale / denom, 0.0), axis=1, keepdims=True
    )
    dtmp[...] = jnp.zeros((16, LANE), F32)
    for c in range(4):
        part = cfull[pl.ds(c, 32, stride=16), :] + cfull[pl.ds(4 + c, 32, stride=16), :]
        row = jnp.sum(weight * part, axis=0, keepdims=True)
        high = row.astype(BF16).astype(F32)
        dtmp[c : c + 1, :] = high
        dtmp[4 + c : 5 + c, :] = row - high
        dtmp[8 + c : 9 + c, :] = jnp.sum(
            cfull[pl.ds(8 + c, 32, stride=16), :], axis=0, keepdims=True
        )
    dsend[...] = dtmp[...].astype(BF16)

    drows = pl.ds(pl.multiple_of(q * 16, 16), 16)
    dlanes = pl.ds(pl.multiple_of(source * LANE, LANE), LANE)

    for dy, dx, dc in ALONG_SEQ[::-1]:
        pltpu.make_async_remote_copy(
            src_ref=dsend,
            dst_ref=drecv.at[drows, dlanes],
            send_sem=send_sem.at[3],
            recv_sem=d_sem.at[(4 - dy) % 4],
            device_id=(at_offset(dy, dx, dc), z),
            device_id_type=MESH,
        ).start()

    drecv[drows, dlanes] = dsend[...]

    at = iota((96, 64), 0)
    c_of, j = at // 24, lax.rem(at, 24)
    part_of = jnp.where(j < 8, 0, jnp.where(j < 16, 8, 4))
    want = lax.rem(j, 4) * 16 + part_of + c_of
    pick = jnp.where(iota((96, 64), 1) == want, 1.0, 0.0).astype(BF16)

    hidden = act_grad = None
    for g in (0, 1, 3, 2):
        come = csend.at[pl.ds(0, 16 * (7 if g == 0 else 8))]
        pltpu.make_async_copy(come, come, d_sem.at[g]).wait()
        first = lax.rem(y + g, 4) * 2
        lanes = pl.ds(pl.multiple_of(first * LANE, 2 * LANE), 2 * LANE)
        picked = nn(pick, drecv[:, lanes])
        strips = []
        for b in range(2):
            for c in range(4):
                strips.append(picked[c * 24 : c * 24 + 24, b * LANE : (b + 1) * LANE])
        strip = jnp.concatenate(strips, axis=1)
        features = pl.ds(pl.multiple_of(first * 512, 1024), 1024)
        rows_f[:, features] = strip
        left = strip[0:16].astype(BF16)
        h, a = nn(left, wiv[0, features, :]), nn(left, wot[features, :])
        hidden, act_grad = (h, a) if hidden is None else (hidden + h, act_grad + a)
    hidden, act_grad = hidden[0:8], act_grad[8:16]
    lhs = rows_f[0:16, :].astype(BF16)
    inner = slope_coef * (hidden + cubic_coef * hidden * hidden * hidden)
    tangent = jnp.tanh(inner)
    active = 0.5 * hidden * (1.0 + tangent)
    slope = 0.5 * (1.0 + tangent) + 0.5 * hidden * (1.0 - tangent * tangent) * slope_coef * (
        1.0 + 3.0 * cubic_coef * hidden * hidden
    )
    pre = act_grad * slope
    upper = iota((8, 256), 0) < 4
    none = jnp.zeros((8, 256), F32)
    active = jnp.where(upper, active, 0.0)
    pre = jnp.where(upper, 0.0, pre)
    active_lo = jnp.concatenate([active, none], axis=0).astype(BF16)
    active_hi = jnp.concatenate([none, active], axis=0).astype(BF16)
    pre_lo = jnp.concatenate([pre, none], axis=0).astype(BF16)
    result = (nn(active_lo, wov[0]) + nn(pre_lo, wit[...]))[0:8]
    wide = iota((8, 4096), 0) < 4
    product = result * (rows_f[0:8, :] + rows_f[16:24, :])
    dots = product[:, 0:LANE]
    for k in range(1, 32):
        dots = dots + product[:, k * LANE : (k + 1) * LANE]
    dots_high = dots.astype(BF16).astype(F32)
    high = result.astype(BF16).astype(F32)
    rest = pltpu.roll(result - high, 4, 0)
    esend[...] = jnp.concatenate(
        [high, jnp.where(wide, rest, jnp.concatenate([dots_high, dots - dots_high] * 16, axis=1))], axis=0
    ).astype(BF16)

    def block(qq, e):
        return esend.at[:, pl.ds(pl.multiple_of((e * 4 + qq) * LANE, LANE), LANE)]

    scatter(block, erecv.at[r], 4)

    grad_w_out[0] = tn(active_hi, lhs).astype(BF16)
    grad_w_in[0] = tn(lhs, pre_lo).astype(BF16)
    for i in range(2):
        pvt[i] = pv[i].T
        gvt[i] = gv[i].T

    arrived(erecv, 4)
    total = erecv[0].astype(F32)
    for k in range(1, NS):
        total = total + erecv[k].astype(F32)
    lower = iota((8, LANE), 0) < 4
    rest = pltpu.roll(total[8:16], 4, 0)
    high = rest.astype(BF16).astype(F32)
    fsend[...] = jnp.concatenate(
        [jnp.where(lower, total[0:8], total[0:8] + rest), jnp.where(lower, high, pltpu.roll(rest - high, 4, 0))], axis=0
    ).astype(BF16)

    frows = pl.ds(pl.multiple_of(source * 16, 16), 16)
    flanes = pl.ds(pl.multiple_of(q * LANE, LANE), LANE)

    for d in ALONG_SEQ[::-1]:
        remote(fsend, frecv.at[frows, flanes], 5, at_offset(*d), z).start()

    frecv[frows, flanes] = fsend[...]

    at = iota((96, LANE), 0)
    kind, slot = at // 32, lax.rem(at, 16)
    want = (slot // 2) * 16 + kind * 4 + (lax.rem(at, 32) // 16) * 2 + lax.rem(slot, 2)
    col = iota((96, LANE), 1)
    again = (kind == 2) & (col == want + 4)
    pick = jnp.where((col == want) | again, 1.0, 0.0).astype(BF16)

    arrived(fwait, 5)
    picked = nn(pick[0:64], frecv[...])
    slot_out = picked[0:32].astype(BF16)
    input_grad = picked[32:64].astype(BF16)
    for i in range(2):
        rows = slice(i * 16, i * 16 + 16)
        comb_part = nn(slot_out[rows], gvt[i])
        disp_part = nn(input_grad[rows], pvt[i])
        for b in range(4):
            lanes = slice(b * LANE, (b + 1) * LANE)
            gsend[i * 4 + b, 0:16] = comb_part[:, lanes].astype(BF16)
            gsend[i * 4 + b, 16:32] = disp_part[:, lanes].astype(BF16)

    for d in ALONG_EXP:
        zz = along(d)
        remote(gsend.at[zz], grecv.at[z], 6, r, zz).start()

    grecv[z] = gsend[z]
    dots = jnp.sum(nn(pick[64:96], frecv[:, 0 : 2 * LANE]), axis=1, keepdims=True)
    dots_b[...] = jnp.broadcast_to(dots, (32, LANE))
    chunk = logit[z]
    ec = jnp.exp(chunk - jnp.max(chunk, axis=0, keepdims=True))
    combine = ec / jnp.sum(ec, axis=0, keepdims=True)
    image = pl.ds(pl.multiple_of((z // 4) * 16, 16), 16)
    dispatch = jnp.exp(chunk - lse_b[image, :])
    col_dots = dots_b[image, :]
    arrived(grecv.at[pl.ds(0, NZ - 1)], 6)
    total = grecv[0].astype(F32)
    for k in range(1, NZ):
        total = total + grecv[k].astype(F32)
    comb_grad, disp_grad = total[0:16], total[16:32]
    row_dots = jnp.sum(combine * comb_grad, axis=0, keepdims=True)
    hbuf[z] = (combine * (comb_grad - row_dots) + dispatch * (disp_grad - col_dots)).astype(BF16)

    for d in ALONG_EXP:
        zz = along(d)
        remote(hbuf.at[z], hbuf.at[z], 7, r, zz).start()

    dispatch_b = []
    for i in range(2):
        li = jnp.concatenate([logit[i * 4 + b] for b in range(4)], axis=1)
        dispatch_b.append(jnp.exp(li - lse_col[i * 16 : i * 16 + 16]).astype(BF16))
    arrived(hbuf.at[pl.ds(0, NZ - 1)], 7)
    logit_b = [
        jnp.concatenate([hbuf[i * 4 + b] for b in range(4)], axis=1) for i in range(2)
    ]
    phi_part = nn(logit_b[0], pv[0]) + nn(logit_b[1], pv[1])
    for h in range(2):
        slots = slice(h * 8, h * 8 + 8)
        pair[h] = jnp.concatenate([phi_part[slots, 0:256], phi_part[slots, 256:512]], axis=0)

    def spread_patches(i):
        left = jnp.concatenate([dispatch_b[i], logit_b[i]], axis=0)
        right = jnp.concatenate([input_grad[i * 16 : i * 16 + 16], phi], axis=0)
        grad_patches[i] = tn(left, right).astype(BF16)

    trade = remote(pair.at[1 - core], paired, 8, sibling, z)
    trade.start()
    spread_patches(0)
    trade.wait_recv()
    half_sum = pair[core] + paired[...]
    isend[...] = half_sum.astype(BF16)
    for dy, dx in CHIPS[:-1]:
        remote(isend, irecv.at[r // 2], 9, at_offset(dy, dx, 0), z).start()
    irecv[r // 2] = isend[...]
    spread_patches(1)
    arrived(irecv.at[pl.ds(0, 15)], 9)
    total = irecv[0].astype(F32)
    for k in range(1, 16):
        total = total + irecv[k].astype(F32)
    halves[core] = total * (1.0 / math.sqrt(2 * 512 * NS))
    back = remote(halves.at[core], halves.at[core], 10, sibling, z)
    back.start()
    sent(asend.at[pl.ds(0, NZ - 1)], 0)
    sent(logit.at[pl.ds(0, NZ - 1)], 1)
    sent(dwait, 3)
    sent(fwait, 5)
    sent(gsend.at[pl.ds(0, NZ - 1)], 6)
    sent(hbuf.at[pl.ds(0, NZ - 1)], 7)
    trade.wait_send()
    sent(irecv.at[pl.ds(0, 15)], 9)

    @pl.when(source == z)
    def _():
        sent(crecv.at[pl.ds(0, 16 * (NS - 1))], 2)
        sent(erecv.at[pl.ds(0, NS - 1)], 4)

    @pl.when(source != z)
    def _():
        sent(crecv, 2)
        sent(erecv, 4)

    back.wait()
    for h in range(2):
        grad_phi[h * 8 : h * 8 + 8, 0:256] = halves[h, 0:8]
        grad_phi[h * 8 : h * 8 + 8, 256:512] = halves[h, 8:16]


def store_kernel(gp, gphi, gwi, gwo, gp_out, gphi_out, gwi_out, gwo_out, sem):
    pieces = [(gphi, gphi_out)]
    for k in range(4):
        rows = pl.ds(k * 1024, 1024)
        pieces.append((gwi.at[:, rows], gwi_out.at[:, rows]))
        rows = pl.ds(k * 64, 64)
        pieces.append((gwo.at[:, rows], gwo_out.at[:, rows]))
    for k in range(2):
        pieces.append((gp.at[k], gp_out.at[k]))
    copies = [
        pltpu.make_async_copy(src, dst, sem.at[k]) for k, (src, dst) in enumerate(pieces)
    ]
    for copy in copies:
        copy.start()
    for copy in copies:
        copy.wait()


def local(patches, grad_out, phi_t, w_in, w_out):
    anywhere = pl.BlockSpec(memory_space=pl.ANY)
    hbm = pl.BlockSpec(memory_space=pltpu.HBM)

    def held(arrays, space):
        return [pltpu.with_memory_space_constraint(a, space) for a in arrays]

    vmem = pltpu.VMEM
    shapes = (
        jax.ShapeDtypeStruct(patches.shape, BF16),
        jax.ShapeDtypeStruct(phi_t.shape, F32),
        jax.ShapeDtypeStruct(w_in.shape, BF16),
        jax.ShapeDtypeStruct(w_out.shape, BF16),
    )
    results = pl.pallas_call(
        kernel,
        out_shape=shapes,
        in_specs=[hbm] * 5,
        out_specs=[pl.BlockSpec(memory_space=pltpu.VMEM)] * 4,
        scratch_shapes=[
            vmem((2, 512, 512), BF16),
            vmem((2, 512, 512), BF16),
            vmem((16, 512), BF16),
            vmem((1, 4096, 256), BF16),
            vmem((1, 256, 4096), BF16),
            vmem((2, 512, 512), BF16),
            vmem((2, 512, 512), BF16),
            vmem((256, 4096), BF16),
            vmem((4096, 256), BF16),
            vmem((8, 16, LANE), F32),
            vmem((8, 16, LANE), F32),
            vmem((8, 16, LANE), F32),
            vmem((512, LANE), F32),
            vmem((512, LANE), BF16),
            vmem((512, LANE), BF16),
            vmem((16, LANE), F32),
            vmem((16, LANE), BF16),
            vmem((64, 1024), BF16),
            vmem((24, 4096), F32),
            vmem((16, 4096), BF16),
            vmem((32, 16, LANE), BF16),
            vmem((16, LANE), BF16),
            vmem((LANE, 512), BF16),
            vmem((32, LANE), F32),
            vmem((32, LANE), F32),
            vmem((8, 32, LANE), BF16),
            vmem((8, 32, LANE), BF16),
            vmem((8, 16, LANE), BF16),
            vmem((2, 16, 256), F32),
            vmem((16, 256), F32),
            vmem((16, 256), BF16),
            vmem((16, 16, 256), BF16),
            vmem((2, 16, 256), F32),
            pltpu.SemaphoreType.DMA((6,)),
            pltpu.SemaphoreType.DMA((11,)),
            pltpu.SemaphoreType.DMA((11,)),
            pltpu.SemaphoreType.DMA((4,)),
            pltpu.SemaphoreType.REGULAR((3,)),
        ],
        compiler_params=pltpu.CompilerParams(
            collective_id=0, has_side_effects=True, vmem_limit_bytes=28 * 1024 * 1024
        ),
        cost_estimate=pl.CostEstimate(
            flops=400_000_000, bytes_accessed=12_000_000, transcendentals=100_000
        ),
    )(*held((patches, grad_out, phi_t, w_in, w_out), pltpu.HBM))
    return pl.pallas_call(
        store_kernel,
        out_shape=shapes,
        in_specs=[anywhere] * 4,
        out_specs=[hbm] * 4,
        scratch_shapes=[pltpu.SemaphoreType.DMA((11,))],
        compiler_params=pltpu.CompilerParams(vmem_limit_bytes=4 * 1024 * 1024),
    )(*held(results, pltpu.VMEM))


def solution(mesh):
    in_specs = (
        P(None, "seq", "exp"),
        P(None, "seq", "exp"),
        P(None, "exp"),
        P("exp", None, "seq"),
        P("exp", "seq", None),
    )
    out_specs = (
        P(None, "seq", "exp"),
        P(None, "exp"),
        P("exp", None, "seq"),
        P("exp", "seq", None),
    )
    return jax.shard_map(local, mesh=mesh, in_specs=in_specs, out_specs=out_specs, check_vma=False)
```

```python
import math

import jax
import jax.numpy as jnp
from jax import lax
from jax.experimental import pallas as pl
from jax.experimental.pallas import tpu as pltpu
from jax.sharding import PartitionSpec as P

MESH = pl.DeviceIdType.MESH
F32 = jnp.float32
BF16 = jnp.bfloat16

slope_coef = 0.7978845608
cubic_coef = 0.044715

NS = 32
NZ = 8
LANE = 128


def ring(d, n):
    return min(d, n - d)


ALONG_EXP = sorted(range(1, NZ), key=lambda d: -ring(d, NZ))
CHIPS = sorted(
    ((dy, dx) for dy in range(4) for dx in range(4)), key=lambda d: -ring(d[0], 4) - ring(d[1], 4)
)
ALONG_SEQ = [(dy, dx, dc) for dy, dx in CHIPS for dc in range(2) if (dy, dx, dc) != (0, 0, 0)]


def nn(a, b):
    return lax.dot_general(a, b, (((1,), (0,)), ((), ())), preferred_element_type=F32)


def nt(a, b):
    return lax.dot_general(a, b, (((1,), (1,)), ((), ())), preferred_element_type=F32)


def tn(a, b):
    return lax.dot_general(a, b, (((0,), (0,)), ((), ())), preferred_element_type=F32)


def iota(shape, dim):
    return lax.broadcasted_iota(jnp.int32, shape, dim)


def thirds(value):
    first = value.astype(BF16).astype(F32)
    second = (value - first).astype(BF16).astype(F32)
    return first, second, value - first - second


def kernel(
    patches, grad_out, phi_t, w_in, w_out,
    grad_patches, grad_phi, grad_w_in, grad_w_out,
    pv, gv, phv, wiv, wov, pvt, gvt, wit, wot,
    asend, arecv, logit, cfull, csend, crecv, dtmp, dsend, drecv, rows_f,
    esend, erecv, fsend, frecv, lse_b, dots_b, gsend, grecv, hbuf, pair, paired, isend, irecv, halves,
    in_sem, send_sem, recv_sem, d_sem, known,
):
    r = lax.axis_index("seq")
    z = lax.axis_index("exp")
    source, q = r // 4, lax.rem(r, 4)

    y, x, core = r // 8, lax.rem(r // 2, 4), lax.rem(r, 2)

    def at_offset(dy, dx, dc):
        return (lax.rem(y + dy, 4) * 4 + lax.rem(x + dx, 4)) * 2 + lax.rem(core + dc, 2)

    def along(d):
        return lax.rem(z + jnp.where(core == 0, d, NZ - d), NZ)

    loads = [
        pltpu.make_async_copy(src, dst, in_sem.at[k])
        for k, (src, dst) in enumerate(
            [
                (phi_t, phv), (patches.at[0], pv.at[0]), (patches.at[1], pv.at[1]),
                (grad_out, gv), (w_out, wov), (w_in, wiv),
            ]
        )
    ]
    for load in loads[:3]:
        load.start()

    barrier = pltpu.get_barrier_semaphore()

    def greet(rr, zz):
        pl.semaphore_signal(barrier, inc=1, device_id=(rr, zz), device_id_type=MESH)

    x_line = [at_offset(0, d, 0) for d in (2, 1, 3)]
    y_line = [at_offset(d, 0, 0) for d in (2, 1, 3)]
    sibling = at_offset(0, 0, 1)

    for d in ALONG_EXP:
        greet(r, lax.rem(z + d, NZ))
    for rr in x_line + y_line + [sibling]:
        greet(rr, z)

    def tell(line, step):
        for rr in line:
            pl.semaphore_signal(known.at[step], inc=1, device_id=(rr, z), device_id_type=MESH)

    def remote(src, dst, phase, rr, zz):
        return pltpu.make_async_remote_copy(
            src_ref=src,
            dst_ref=dst,
            send_sem=send_sem.at[phase],
            recv_sem=recv_sem.at[phase],
            device_id=(rr, zz),
            device_id_type=MESH,
        )

    def arrived(ref, phase):
        pltpu.make_async_copy(ref, ref, recv_sem.at[phase]).wait()

    dwait = fwait = csend.at[pl.ds(0, 16 * (NS - 1))]

    def sent(ref, phase):
        pltpu.make_async_copy(ref, ref, send_sem.at[phase]).wait()

    def scatter(piece, place, phase):
        for d in ALONG_EXP:
            e = lax.rem(z + d, NZ)
            for k in range(4):
                qq = lax.rem(r + k, 4)
                remote(piece(qq, e), place, phase, z * 4 + qq, e).start()
        for k in range(4):
            qq = lax.rem(r + k, 4)
            rr = z * 4 + qq

            @pl.when(rr != r)
            def _():
                remote(piece(qq, z), place, phase, rr, z).start()

            @pl.when(rr == r)
            def _():
                pltpu.make_async_copy(piece(qq, z), place, recv_sem.at[phase]).start()

    loads[0].wait()
    phi = phv[...]
    for i in range(2):
        loads[1 + i].wait()
        part = nt(phi, pv[i])
        for b in range(4):
            asend[i * 4 + b] = part[:, b * LANE : (b + 1) * LANE]
    for load in loads[3:]:
        load.start()

    pl.semaphore_wait(barrier, NZ - 1 + 7)

    for d in ALONG_EXP:
        zz = along(d)
        remote(asend.at[zz], arecv.at[z], 0, r, zz).start()

    arecv[z] = asend[z]
    tell([sibling], 0)
    pl.semaphore_wait(known.at[0], 1)
    tell(x_line, 1)
    arrived(arecv.at[pl.ds(0, NZ - 1)], 0)
    total = arecv[0]
    for k in range(1, NZ):
        total = total + arecv[k]
    logit[z] = total

    for d in ALONG_EXP:
        zz = along(d)
        remote(logit.at[z], logit.at[z], 1, r, zz).start()

    pl.semaphore_wait(known.at[1], 3)
    tell(y_line, 2)
    loads[3].wait()
    arrived(logit.at[pl.ds(0, NZ - 1)], 1)
    pl.semaphore_wait(known.at[2], 3)

    diag = iota((32, LANE), 0) == iota((32, LANE), 1)
    peaks, sums = [], []
    for i in range(2):
        li = jnp.concatenate([logit[i * 4 + b] for b in range(4)], axis=1)
        peak = jnp.max(li, axis=1, keepdims=True).astype(BF16).astype(F32)
        e = jnp.exp(li - peak)
        peaks.append(peak)
        sums.append(jnp.sum(e, axis=1, keepdims=True))
        hi = e.astype(BF16)
        lo = (e - hi.astype(F32)).astype(BF16)
        both = nn(jnp.concatenate([hi, lo], axis=0), pv[i])
        slot_part = both[:16] + both[16:]
        ec = jnp.exp(li - jnp.max(li, axis=0, keepdims=True))
        combine_b = (ec / jnp.sum(ec, axis=0, keepdims=True)).astype(BF16)
        grad_part = nn(combine_b, gv[i])
        for half in range(2):
            for c in range(4):
                base = (i * 16 + half * 8) * 16 + c
                rows = slice(half * 8, half * 8 + 8)
                lanes = slice(c * LANE, (c + 1) * LANE)
                high = slot_part[rows, lanes].astype(BF16).astype(F32)
                cfull[pl.ds(base, 8, stride=16), :] = high
                cfull[pl.ds(base + 4, 8, stride=16), :] = slot_part[rows, lanes] - high
                cfull[pl.ds(base + 8, 8, stride=16), :] = grad_part[rows, lanes]
    peak_col = jnp.concatenate(peaks, axis=0)
    sum_col = jnp.concatenate(sums, axis=0)
    peak_row = jnp.sum(jnp.where(diag, peak_col, 0.0), axis=0, keepdims=True)
    sum_row = jnp.sum(jnp.where(diag, sum_col, 0.0), axis=0, keepdims=True)
    stats = (peak_row,) + thirds(sum_row)
    for k, row in enumerate(stats):
        cfull[pl.ds(12 + k, 32, stride=16), :] = jnp.broadcast_to(row, (32, LANE))
    csend[...] = cfull[...].astype(BF16)

    def piece(qq, e):
        row = (qq // 2) * 16 + e * 2 + lax.rem(qq, 2)
        return csend.at[pl.ds(pl.multiple_of(row * 16, 16), 16)]

    scatter(piece, crecv.at[pl.ds(pl.multiple_of(r * 16, 16), 16)], 2)
    loads[4].wait()
    wot[...] = wov[0].T
    loads[5].wait()
    wit[...] = wiv[0].T
    arrived(crecv, 2)
    cfull[...] = crecv[...].astype(F32)
    peak_all = cfull[pl.ds(12, 32, stride=16), :]
    sum_all = (
        cfull[pl.ds(13, 32, stride=16), :]
        + cfull[pl.ds(14, 32, stride=16), :]
        + cfull[pl.ds(15, 32, stride=16), :]
    )
    top = jnp.max(peak_all, axis=0, keepdims=True)
    scale = jnp.exp(peak_all - top)
    denom = jnp.sum(scale * sum_all, axis=0, keepdims=True)
    lse_row = top + jnp.log(denom)
    lse_col = jnp.sum(jnp.where(diag, lse_row, 0.0), axis=1, keepdims=True)
    lse_b[...] = jnp.broadcast_to(lse_col, (32, LANE))
    mine = (q // 2) * 16 + z * 2 + lax.rem(q, 2)
    weight = jnp.sum(
        jnp.where(iota((32, LANE), 1) == mine, scale / denom, 0.0), axis=1, keepdims=True
    )
    dtmp[...] = jnp.zeros((16, LANE), F32)
    for c in range(4):
        part = cfull[pl.ds(c, 32, stride=16), :] + cfull[pl.ds(4 + c, 32, stride=16), :]
        row = jnp.sum(weight * part, axis=0, keepdims=True)
        high = row.astype(BF16).astype(F32)
        dtmp[c : c + 1, :] = high
        dtmp[4 + c : 5 + c, :] = row - high
        dtmp[8 + c : 9 + c, :] = jnp.sum(
            cfull[pl.ds(8 + c, 32, stride=16), :], axis=0, keepdims=True
        )
    dsend[...] = dtmp[...].astype(BF16)

    drows = pl.ds(pl.multiple_of(q * 16, 16), 16)
    dlanes = pl.ds(pl.multiple_of(source * LANE, LANE), LANE)

    for dy, dx, dc in ALONG_SEQ[::-1]:
        pltpu.make_async_remote_copy(
            src_ref=dsend,
            dst_ref=drecv.at[drows, dlanes],
            send_sem=send_sem.at[3],
            recv_sem=d_sem.at[(4 - dy) % 4],
            device_id=(at_offset(dy, dx, dc), z),
            device_id_type=MESH,
        ).start()

    drecv[drows, dlanes] = dsend[...]

    at = iota((96, 64), 0)
    c_of, j = at // 24, lax.rem(at, 24)
    part_of = jnp.where(j < 8, 0, jnp.where(j < 16, 8, 4))
    want = lax.rem(j, 4) * 16 + part_of + c_of
    pick = jnp.where(iota((96, 64), 1) == want, 1.0, 0.0).astype(BF16)

    hidden = act_grad = None
    for g in (0, 1, 3, 2):
        come = csend.at[pl.ds(0, 16 * (7 if g == 0 else 8))]
        pltpu.make_async_copy(come, come, d_sem.at[g]).wait()
        first = lax.rem(y + g, 4) * 2
        lanes = pl.ds(pl.multiple_of(first * LANE, 2 * LANE), 2 * LANE)
        picked = nn(pick, drecv[:, lanes])
        strips = []
        for b in range(2):
            for c in range(4):
                strips.append(picked[c * 24 : c * 24 + 24, b * LANE : (b + 1) * LANE])
        strip = jnp.concatenate(strips, axis=1)
        features = pl.ds(pl.multiple_of(first * 512, 1024), 1024)
        rows_f[:, features] = strip
        left = strip[0:16].astype(BF16)
        h, a = nn(left, wiv[0, features, :]), nn(left, wot[features, :])
        hidden, act_grad = (h, a) if hidden is None else (hidden + h, act_grad + a)
    hidden, act_grad = hidden[0:8], act_grad[8:16]
    lhs = rows_f[0:16, :].astype(BF16)
    inner = slope_coef * (hidden + cubic_coef * hidden * hidden * hidden)
    tangent = jnp.tanh(inner)
    active = 0.5 * hidden * (1.0 + tangent)
    slope = 0.5 * (1.0 + tangent) + 0.5 * hidden * (1.0 - tangent * tangent) * slope_coef * (
        1.0 + 3.0 * cubic_coef * hidden * hidden
    )
    pre = act_grad * slope
    upper = iota((8, 256), 0) < 4
    none = jnp.zeros((8, 256), F32)
    active = jnp.where(upper, active, 0.0)
    pre = jnp.where(upper, 0.0, pre)
    active_lo = jnp.concatenate([active, none], axis=0).astype(BF16)
    active_hi = jnp.concatenate([none, active], axis=0).astype(BF16)
    pre_lo = jnp.concatenate([pre, none], axis=0).astype(BF16)
    result = (nn(active_lo, wov[0]) + nn(pre_lo, wit[...]))[0:8]
    wide = iota((8, 4096), 0) < 4
    product = result * (rows_f[0:8, :] + rows_f[16:24, :])
    dots = product[:, 0:LANE]
    for k in range(1, 32):
        dots = dots + product[:, k * LANE : (k + 1) * LANE]
    dots_high = dots.astype(BF16).astype(F32)
    high = result.astype(BF16).astype(F32)
    rest = pltpu.roll(result - high, 4, 0)
    esend[...] = jnp.concatenate(
        [high, jnp.where(wide, rest, jnp.concatenate([dots_high, dots - dots_high] * 16, axis=1))], axis=0
    ).astype(BF16)

    def block(qq, e):
        return esend.at[:, pl.ds(pl.multiple_of((e * 4 + qq) * LANE, LANE), LANE)]

    scatter(block, erecv.at[r], 4)

    grad_w_out[0] = tn(active_hi, lhs).astype(BF16)
    grad_w_in[0] = tn(lhs, pre_lo).astype(BF16)
    for i in range(2):
        pvt[i] = pv[i].T
        gvt[i] = gv[i].T

    arrived(erecv, 4)
    total = erecv[0].astype(F32)
    for k in range(1, NS):
        total = total + erecv[k].astype(F32)
    lower = iota((8, LANE), 0) < 4
    rest = pltpu.roll(total[8:16], 4, 0)
    high = rest.astype(BF16).astype(F32)
    fsend[...] = jnp.concatenate(
        [jnp.where(lower, total[0:8], total[0:8] + rest), jnp.where(lower, high, pltpu.roll(rest - high, 4, 0))], axis=0
    ).astype(BF16)

    frows = pl.ds(pl.multiple_of(source * 16, 16), 16)
    flanes = pl.ds(pl.multiple_of(q * LANE, LANE), LANE)

    for d in ALONG_SEQ[::-1]:
        remote(fsend, frecv.at[frows, flanes], 5, at_offset(*d), z).start()

    frecv[frows, flanes] = fsend[...]

    at = iota((96, LANE), 0)
    kind, slot = at // 32, lax.rem(at, 16)
    want = (slot // 2) * 16 + kind * 4 + (lax.rem(at, 32) // 16) * 2 + lax.rem(slot, 2)
    col = iota((96, LANE), 1)
    again = (kind == 2) & (col == want + 4)
    pick = jnp.where((col == want) | again, 1.0, 0.0).astype(BF16)

    arrived(fwait, 5)
    picked = nn(pick[0:64], frecv[...])
    slot_out = picked[0:32].astype(BF16)
    input_grad = picked[32:64].astype(BF16)
    for i in range(2):
        rows = slice(i * 16, i * 16 + 16)
        comb_part = nn(slot_out[rows], gvt[i])
        disp_part = nn(input_grad[rows], pvt[i])
        for b in range(4):
            lanes = slice(b * LANE, (b + 1) * LANE)
            gsend[i * 4 + b, 0:16] = comb_part[:, lanes].astype(BF16)
            gsend[i * 4 + b, 16:32] = disp_part[:, lanes].astype(BF16)

    for d in ALONG_EXP:
        zz = along(d)
        remote(gsend.at[zz], grecv.at[z], 6, r, zz).start()

    grecv[z] = gsend[z]
    dots = jnp.sum(nn(pick[64:96], frecv[:, 0 : 2 * LANE]), axis=1, keepdims=True)
    dots_b[...] = jnp.broadcast_to(dots, (32, LANE))
    chunk = logit[z]
    ec = jnp.exp(chunk - jnp.max(chunk, axis=0, keepdims=True))
    combine = ec / jnp.sum(ec, axis=0, keepdims=True)
    image = pl.ds(pl.multiple_of((z // 4) * 16, 16), 16)
    dispatch = jnp.exp(chunk - lse_b[image, :])
    col_dots = dots_b[image, :]
    arrived(grecv.at[pl.ds(0, NZ - 1)], 6)
    total = grecv[0].astype(F32)
    for k in range(1, NZ):
        total = total + grecv[k].astype(F32)
    comb_grad, disp_grad = total[0:16], total[16:32]
    row_dots = jnp.sum(combine * comb_grad, axis=0, keepdims=True)
    hbuf[z] = (combine * (comb_grad - row_dots) + dispatch * (disp_grad - col_dots)).astype(BF16)

    for d in ALONG_EXP:
        zz = along(d)
        remote(hbuf.at[z], hbuf.at[z], 7, r, zz).start()

    dispatch_b = []
    for i in range(2):
        li = jnp.concatenate([logit[i * 4 + b] for b in range(4)], axis=1)
        dispatch_b.append(jnp.exp(li - lse_col[i * 16 : i * 16 + 16]).astype(BF16))
    arrived(hbuf.at[pl.ds(0, NZ - 1)], 7)
    logit_b = [
        jnp.concatenate([hbuf[i * 4 + b] for b in range(4)], axis=1) for i in range(2)
    ]
    phi_part = nn(logit_b[0], pv[0]) + nn(logit_b[1], pv[1])
    for h in range(2):
        slots = slice(h * 8, h * 8 + 8)
        pair[h] = jnp.concatenate([phi_part[slots, 0:256], phi_part[slots, 256:512]], axis=0)

    def spread_patches(i):
        left = jnp.concatenate([dispatch_b[i], logit_b[i]], axis=0)
        right = jnp.concatenate([input_grad[i * 16 : i * 16 + 16], phi], axis=0)
        grad_patches[i] = tn(left, right).astype(BF16)

    trade = remote(pair.at[1 - core], paired, 8, sibling, z)
    trade.start()
    spread_patches(0)
    trade.wait_recv()
    half_sum = pair[core] + paired[...]
    isend[...] = half_sum.astype(BF16)
    for dy, dx in CHIPS[-2::-1]:
        remote(isend, irecv.at[r // 2], 9, at_offset(dy, dx, 0), z).start()
    irecv[r // 2] = isend[...]
    spread_patches(1)
    arrived(irecv.at[pl.ds(0, 15)], 9)
    total = irecv[0].astype(F32)
    for k in range(1, 16):
        total = total + irecv[k].astype(F32)
    halves[core] = total * (1.0 / math.sqrt(2 * 512 * NS))
    back = remote(halves.at[core], halves.at[core], 10, sibling, z)
    back.start()
    sent(asend.at[pl.ds(0, NZ - 1)], 0)
    sent(logit.at[pl.ds(0, NZ - 1)], 1)
    sent(dwait, 3)
    sent(fwait, 5)
    sent(gsend.at[pl.ds(0, NZ - 1)], 6)
    sent(hbuf.at[pl.ds(0, NZ - 1)], 7)
    trade.wait_send()
    sent(irecv.at[pl.ds(0, 15)], 9)

    @pl.when(source == z)
    def _():
        sent(crecv.at[pl.ds(0, 16 * (NS - 1))], 2)
        sent(erecv.at[pl.ds(0, NS - 1)], 4)

    @pl.when(source != z)
    def _():
        sent(crecv, 2)
        sent(erecv, 4)

    back.wait()
    for h in range(2):
        grad_phi[h * 8 : h * 8 + 8, 0:256] = halves[h, 0:8]
        grad_phi[h * 8 : h * 8 + 8, 256:512] = halves[h, 8:16]


def store_kernel(gp, gphi, gwi, gwo, gp_out, gphi_out, gwi_out, gwo_out, sem):
    pieces = [(gphi, gphi_out)]
    for k in range(2):
        rows = pl.ds(k * 2048, 2048)
        pieces.append((gwi.at[:, rows], gwi_out.at[:, rows]))
        rows = pl.ds(k * 128, 128)
        pieces.append((gwo.at[:, rows], gwo_out.at[:, rows]))
    for k in range(2):
        pieces.append((gp.at[k], gp_out.at[k]))
    copies = [
        pltpu.make_async_copy(src, dst, sem.at[k]) for k, (src, dst) in enumerate(pieces)
    ]
    for copy in copies:
        copy.start()
    for copy in copies:
        copy.wait()


def local(patches, grad_out, phi_t, w_in, w_out):
    anywhere = pl.BlockSpec(memory_space=pl.ANY)
    hbm = pl.BlockSpec(memory_space=pltpu.HBM)

    def held(arrays, space):
        return [pltpu.with_memory_space_constraint(a, space) for a in arrays]

    vmem = pltpu.VMEM
    shapes = (
        jax.ShapeDtypeStruct(patches.shape, BF16),
        jax.ShapeDtypeStruct(phi_t.shape, F32),
        jax.ShapeDtypeStruct(w_in.shape, BF16),
        jax.ShapeDtypeStruct(w_out.shape, BF16),
    )
    results = pl.pallas_call(
        kernel,
        out_shape=shapes,
        in_specs=[hbm] * 5,
        out_specs=[pl.BlockSpec(memory_space=pltpu.VMEM)] * 4,
        scratch_shapes=[
            vmem((2, 512, 512), BF16),
            vmem((2, 512, 512), BF16),
            vmem((16, 512), BF16),
            vmem((1, 4096, 256), BF16),
            vmem((1, 256, 4096), BF16),
            vmem((2, 512, 512), BF16),
            vmem((2, 512, 512), BF16),
            vmem((256, 4096), BF16),
            vmem((4096, 256), BF16),
            vmem((8, 16, LANE), F32),
            vmem((8, 16, LANE), F32),
            vmem((8, 16, LANE), F32),
            vmem((512, LANE), F32),
            vmem((512, LANE), BF16),
            vmem((512, LANE), BF16),
            vmem((16, LANE), F32),
            vmem((16, LANE), BF16),
            vmem((64, 1024), BF16),
            vmem((24, 4096), F32),
            vmem((16, 4096), BF16),
            vmem((32, 16, LANE), BF16),
            vmem((16, LANE), BF16),
            vmem((LANE, 512), BF16),
            vmem((32, LANE), F32),
            vmem((32, LANE), F32),
            vmem((8, 32, LANE), BF16),
            vmem((8, 32, LANE), BF16),
            vmem((8, 16, LANE), BF16),
            vmem((2, 16, 256), F32),
            vmem((16, 256), F32),
            vmem((16, 256), BF16),
            vmem((16, 16, 256), BF16),
            vmem((2, 16, 256), F32),
            pltpu.SemaphoreType.DMA((6,)),
            pltpu.SemaphoreType.DMA((11,)),
            pltpu.SemaphoreType.DMA((11,)),
            pltpu.SemaphoreType.DMA((4,)),
            pltpu.SemaphoreType.REGULAR((3,)),
        ],
        compiler_params=pltpu.CompilerParams(
            collective_id=0, has_side_effects=True, vmem_limit_bytes=28 * 1024 * 1024
        ),
        cost_estimate=pl.CostEstimate(
            flops=400_000_000, bytes_accessed=12_000_000, transcendentals=100_000
        ),
    )(*held((patches, grad_out, phi_t, w_in, w_out), pltpu.HBM))
    return pl.pallas_call(
        store_kernel,
        out_shape=shapes,
        in_specs=[anywhere] * 4,
        out_specs=[hbm] * 4,
        scratch_shapes=[pltpu.SemaphoreType.DMA((7,))],
        compiler_params=pltpu.CompilerParams(vmem_limit_bytes=4 * 1024 * 1024),
    )(*held(results, pltpu.VMEM))


def solution(mesh):
    in_specs = (
        P(None, "seq", "exp"),
        P(None, "seq", "exp"),
        P(None, "exp"),
        P("exp", None, "seq"),
        P("exp", "seq", None),
    )
    out_specs = (
        P(None, "seq", "exp"),
        P(None, "exp"),
        P("exp", None, "seq"),
        P("exp", "seq", None),
    )
    return jax.shard_map(local, mesh=mesh, in_specs=in_specs, out_specs=out_specs, check_vma=False)
```
